512 devices in a mesh: dp: 8 (over z_hi, y), shard: 16 (over z_lo, core), seq: 4 (over x).
Axes of the slice: x: 4, y: 4, z: 16 (z_hi: 2, z_lo: 8; z = z_hi * 8 + z_lo), core: 2. Of those that a mesh axis runs over, the one named last changes fastest.
Arguments:
- qkv: bfloat16 [128, 196, 3, 2560], P(('dp', 'shard'), 'seq'), may hold values from -6 to 6
- hidden_in: bfloat16 [128, 196, 5120], P(('dp', 'shard'), 'seq'), may hold values from -6 to 6
- clips: bfloat16 [128, 4, 14, 14, 512], P(('dp', 'shard'), 'seq'), may hold values from -6 to 6
- reset: int32 [128], P(('dp', 'shard')), may hold values 0 or 1
- source_group: int32 [128], P(('dp', 'shard')), may hold values from 0 to 7
- step_index: int32 [128], P(('dp', 'shard')), may hold values from 0 to 34
- conv_weight: bfloat16 [2, 3, 3, 512, 16], replicated, may hold values from -0.0625 to 0.0625
- embed_weight: bfloat16 [64, 5120], replicated, may hold values from -0.75 to 0.75
- out_weight: bfloat16 [2560, 5120], P('seq', 'shard'), may hold values from -0.125 to 0.125
- gate_table: bfloat16 [35, 5120], replicated, may hold values from -8 to 8
Outputs:
- hidden_out: bfloat16 [128, 196, 5120], P(('dp', 'shard'), 'seq')
The draws below stay inside these ranges and needn't reach their ends.
All inputs are finite; a program needn't handle non-finite values. No bound on the sum of `reset` on one device may be relied on, other than what follows from the above.
Results may differ from the reference program's by a relative error of at most 0.012.
Values may be sent and summed in bfloat16 or wider, within the bound.
A program may use at most 64 MiB of HBM per device.

```python
import math
import jax
import jax.numpy as jnp
from jax import lax

D = 5120
HEADS = 20
HD = 128
CC = 512
ZC = 16
LS = 14
STEPS = 35
ENVS = 128
LF = 4
TOKENS_ENV = 196
HW = 2560
N_DP = 8
N_SHARD = 16
N_SEQ = 4


def draw_qkv(key, part):
    key = jax.random.fold_in(key, 11)
    full_shape = (ENVS, TOKENS_ENV, 3, HEADS * HD)
    base_draw = jnp.clip(jax.random.normal(key, full_shape, jnp.float32), -6.0, 6.0)
    return base_draw.astype(jnp.bfloat16)


def set_ends(drawn, own_key, least, top_value):
    dims = drawn.shape
    place = [jax.random.randint(jax.random.fold_in(own_key, axis), (), 0, dims[axis]) for axis in range(len(dims))]
    drawn = drawn.at[tuple(place)].set(least)
    longest = dims.index(max(dims))
    place[longest] = (place[longest] + 1) % dims[longest]
    return drawn.at[tuple(place)].set(top_value)


def level_of(own_key, shape, pieces, smallest, high):
    factor_of, own = 1.0, jax.random.fold_in(own_key, 6)
    for position, parts in pieces:
        draws = jnp.exp(jax.random.uniform(jax.random.fold_in(own, position), (parts,), jnp.float32, smallest / len(pieces), high / len(pieces)))
        factor_of = factor_of * jnp.repeat(draws, shape[position] // parts).reshape([-1 if axis == position else 1 for axis in range(len(shape))])
    return factor_of


def centred(rng, dims, scale, limit, cuts=(), kind=jnp.bfloat16):
    result = jax.random.normal(rng, dims, jnp.float32) * scale
    if len(cuts) > 0:
        result = level_of(rng, dims, cuts, -0.22, 0.18) * result
    return jnp.clip(result, min=-limit, max=limit).astype(kind)


def setup_inputs(seed: int = 0) -> dict:
    key_list = jax.random.split(jax.random.key(seed), 11)
    qkv = draw_qkv(jax.random.fold_in(key_list[10], 71), 0)
    hidden_in = centred(key_list[1], (ENVS, TOKENS_ENV, D), 1.0, 6.0, ((0, 128), (1, 4)))
    clips = centred(key_list[2], (ENVS, LF, LS, LS, CC), 1.0, 6.0, ((0, 128), (1, 4)))
    reset = set_ends((jax.random.randint(key_list[3], (ENVS,), 0, 2) < 1).astype(jnp.int32), jax.random.fold_in(key_list[3], 1), 0, 1)
    source_group = set_ends(jax.random.randint(key_list[4], (ENVS,), 0, N_DP), jax.random.fold_in(key_list[4], 1), 0, N_DP - 1).astype(jnp.int32)
    step_index = set_ends(jax.random.randint(key_list[5], (ENVS,), 0, STEPS), jax.random.fold_in(key_list[5], 1), 0, STEPS - 1).astype(jnp.int32)
    conv_weight = centred(key_list[6], (2, 3, 3, CC, ZC), (18 * CC) ** -0.5, 0.0625)
    embed_weight = centred(key_list[7], (4 * ZC, D), (4 * ZC) ** -0.5, 0.75)
    out_weight = centred(key_list[8], (HW, D), HW ** -0.5, 0.125, ((0, 4), (1, 16)))
    gate_table = centred(key_list[9], (STEPS, D), 2.0, 8.0)
    return {"qkv": qkv, "hidden_in": hidden_in, "clips": clips, "reset": reset, "source_group": source_group, "step_index": step_index, "conv_weight": conv_weight, "embed_weight": embed_weight, "out_weight": out_weight, "gate_table": gate_table}


def patch_tokens(latent):
    frames, grid_side, _, channels = latent.shape
    half_side = grid_side // 2
    grid_cells = latent.reshape(frames, half_side, 2, half_side, 2, channels)
    grid_cells = grid_cells.transpose(0, 1, 3, 2, 4, 5)
    return grid_cells.reshape(frames * half_side * half_side, 4 * channels)

def encode_clip(clip_block, conv_weight):
    activated = jax.nn.silu(clip_block.astype(jnp.float32)).astype(jnp.bfloat16)
    previous = jnp.concatenate([jnp.zeros_like(activated[:1]), activated[:-1]], axis=0)
    stacked = jnp.stack([previous, activated], axis=1)
    grid_side = activated.shape[1]
    padded = jnp.pad(stacked, ((0, 0), (0, 0), (1, 1), (1, 1), (0, 0)))
    tap_list = []
    for delta_t in range(2):
        for delta_y in range(3):
            for delta_x in range(3):
                tap_list.append(padded[:, delta_t, delta_y:delta_y + grid_side, delta_x:delta_x + grid_side, :])
    columns = jnp.concatenate(tap_list, axis=-1)
    flat_columns = columns.reshape(-1, columns.shape[-1])
    weight_matrix = conv_weight.reshape(-1, conv_weight.shape[-1])
    latent = jnp.dot(flat_columns, weight_matrix, preferred_element_type=jnp.float32).astype(jnp.bfloat16)
    return latent.reshape(activated.shape[0], grid_side, grid_side, conv_weight.shape[-1])

def attend_env(qkv_block):
    seq_length, _, head_width = qkv_block.shape
    head_count = head_width // HD
    grouped = qkv_block.reshape(seq_length, 3, head_count, HD).astype(jnp.float32)
    scores = jnp.einsum('qhd,khd->hqk', grouped[:, 0], grouped[:, 1]) / math.sqrt(HD)
    highest = lax.optimization_barrier(jnp.max(scores, axis=-1, keepdims=True))
    powers = jnp.exp(scores - highest)
    weights = (powers / lax.optimization_barrier(jnp.sum(powers, axis=-1, keepdims=True))).astype(jnp.bfloat16)
    mixed = jnp.einsum('hqk,khd->qhd', weights.astype(jnp.float32), grouped[:, 2])
    return mixed.astype(jnp.bfloat16).reshape(seq_length, head_width)

def reference(qkv, hidden_in, clips, reset, source_group, step_index, conv_weight, embed_weight, out_weight, gate_table):
    group_width = HEADS * HD // N_SEQ
    weight_rows = out_weight.reshape(N_SEQ, group_width, -1).astype(jnp.float32)

    def one_env(env_index):
        step_here = lax.dynamic_index_in_dim(step_index, env_index, 0, keepdims=False).astype(jnp.int32)
        gate_row = lax.dynamic_index_in_dim(gate_table, step_here, 0, keepdims=False).astype(jnp.float32)
        source_index = lax.dynamic_index_in_dim(source_group, env_index, 0, keepdims=False) * N_SHARD + env_index % N_SHARD
        clip_block = lax.dynamic_index_in_dim(clips, source_index.astype(jnp.int32), 0, keepdims=False)
        condition = jnp.dot(patch_tokens(encode_clip(clip_block, conv_weight)), embed_weight, preferred_element_type=jnp.float32)
        qkv_block = lax.dynamic_index_in_dim(qkv, env_index, 0, keepdims=False)
        attended = attend_env(qkv_block)
        grouped = attended.reshape(attended.shape[0], N_SEQ, group_width).astype(jnp.float32)
        partials = jnp.einsum('lgc,gcd->gld', grouped, weight_rows).astype(jnp.bfloat16)
        partials = lax.optimization_barrier(partials).astype(jnp.float32)
        projected = lax.optimization_barrier(jnp.sum(partials, axis=0))
        reset_flag = lax.dynamic_index_in_dim(reset, env_index, 0, keepdims=False).astype(jnp.float32)
        residual = lax.dynamic_index_in_dim(hidden_in, env_index, 0, keepdims=False).astype(jnp.float32)
        return (residual + reset_flag * condition + gate_row * projected).astype(jnp.bfloat16)
    return lax.map(one_env, jnp.arange(ENVS, dtype=jnp.int32))
```

```python
import math

import jax
import jax.numpy as jnp
from jax import lax
from jax.experimental import pallas as pl
from jax.experimental.pallas import tpu as pltpu
from jax.sharding import PartitionSpec as P

MESH = pl.DeviceIdType.MESH
BF16, F32 = jnp.bfloat16, jnp.float32
HD = 128
HG = 5
GW = HG * HD
D = 5120
NB = 8
BW = D // NB
CW = BW // 2
ROWS = 48
MAIN = 4 * ROWS
ALL = MAIN + 16
ORDER = (0, 7, 1, 6, 2, 5, 3, 4)
NT = (((1,), (1,)), ((), ()))


def body(
    reset_ref, source_ref, step_ref, qkv_ref, hidden_ref, clip_ref, conv_ref, embed_ref, w_ref, gate_ref,
    out_ref,
    qkv_v, hidden_v, clip_v, conv_v, embed_v, gate_v, out_v,
    wg, heads, tail_out, tail_in, att, terms, recv, tsend, trecv, act, sh, bsend, brecv, packs, gate_row, patch,
    loc_sem, send_sem, head_sem, tail_sem, z_sem, y_sem, sib_sem, term_sem, tt_sem, b_sem, pz_sem, py_sem,
):
    g, s, x = lax.axis_index("dp"), lax.axis_index("shard"), lax.axis_index("seq")
    zh, y, zl, c = g // 4, g % 4, s // 2, s % 2
    z = zh * 8 + zl
    hy = y % 2

    def at_x(d):
        return {"seq": (x + d) % 4}

    def at_y(d):
        return {"dp": zh * 4 + (y + d) % 4}

    def at_z(d):
        zz = (z + d) % 16
        return {"dp": (zz // 8) * 4 + y, "shard": (zz % 8) * 2 + c}

    sibling = {"shard": zl * 2 + 1 - c}
    partner = {"dp": (g + 4) % 8}

    barrier = pltpu.get_barrier_semaphore()
    everyone = [at_x(1), at_x(2), at_x(3), at_z(1), at_z(15), at_y(1), at_y(2), at_y(3), sibling, partner]
    for dev in everyone:
        pl.semaphore_signal(barrier, inc=1, device_id=dev, device_id_type=MESH)

    locals_ = []

    def load(src, dst):
        copy = pltpu.make_async_copy(src, dst, loc_sem.at[len(locals_)])
        copy.start()
        locals_.append(copy)
        return copy

    sent = []

    def send(src, dst, sem, dev):
        copy = pltpu.make_async_remote_copy(
            src_ref=src, dst_ref=dst, send_sem=send_sem.at[len(sent)], recv_sem=sem, device_id=dev, device_id_type=MESH
        )
        copy.start()
        sent.append(copy)

    def arrived(dst, sem):
        pltpu.make_async_remote_copy(
            src_ref=dst, dst_ref=dst, send_sem=send_sem.at[0], recv_sem=sem, device_id=sibling, device_id_type=MESH
        ).wait_recv()

    def block_rows(rel, core):
        return pl.multiple_of(((zl + rel) % 8) * BW + core * CW, 16)

    def cols(rel):
        return pl.ds(pl.multiple_of(((zl + rel) % 8) * BW, 128), BW)

    def w_at(start, size):
        return wg.at[pl.ds(pl.multiple_of(start, 16), size), :]

    qkv_in = load(qkv_ref, qkv_v)
    own_heads = load(
        qkv_ref.at[:, pl.ds(0, ROWS), pl.ds(pl.multiple_of(x * GW, 128), GW)], heads.at[:, pl.ds(0, ROWS), :]
    )
    clip_in = load(clip_ref, clip_v)
    conv_in = load(conv_ref, conv_v)
    own_w = load(w_ref, w_at(block_rows(0, c), CW))
    embed_in = load(embed_ref, embed_v)
    gate_in = load(gate_ref, gate_v)
    hidden_in = load(hidden_ref, hidden_v)

    pl.semaphore_wait(barrier, len(everyone))

    for d in (1, 3, 2):
        send(
            qkv_ref.at[:, pl.ds(0, ROWS), pl.ds(pl.multiple_of(((x + d) % 4) * GW, 128), GW)],
            heads.at[:, pl.ds((4 - d) * ROWS, ROWS), :],
            head_sem.at[4 - d],
            at_x(d),
        )
    half = pl.ds(pl.multiple_of(hy * 160, 16), 160)
    for way, d in ((0, 1), (1, 15)):
        send(w_ref.at[half, :], w_at(block_rows(0, c) + hy * 160, 160), z_sem.at[way, 1], at_z(d))
    send(w_ref, w_at(block_rows(0, c), CW), sib_sem.at[0], sibling)

    qkv_in.wait()
    row16 = lax.broadcasted_iota(jnp.int32, (16, 4 * GW), 0)
    tails = [qkv_v[p, ROWS : ROWS + 1, :].astype(F32) for p in range(3)]
    tail_out[...] = jnp.where(
        row16 == 0, tails[0], jnp.where(row16 == 1, tails[1], jnp.where(row16 == 2, tails[2], 0.0))
    ).astype(BF16)
    for d in (1, 3, 2):
        send(
            tail_out.at[:, pl.ds(pl.multiple_of(((x + d) % 4) * GW, 128), GW)],
            tail_in.at[4 - d],
            tail_sem.at[4 - d],
            at_x(d),
        )

    def w_poll(k):
        for way, d in ((0, 1), (1, 15)):
            rel = (8 - k) if way == 0 else k
            first = block_rows(rel, c) + hy * 160
            if k < 4:
                arrived(w_at(first, 160), z_sem.at[way, k])
                if k < 3:
                    send(w_at(first, 160), w_at(first, 160), z_sem.at[way, k + 1], at_z(d))
                else:
                    q = first + 80 * way
                    send(w_at(q, 80), w_at(q, 80), z_sem.at[way, 4], at_z(d))
                send(w_at(first, 80), w_at(first, 80), y_sem.at[rel], at_y(1))
                send(w_at(first + 80, 80), w_at(first + 80, 80), y_sem.at[rel], at_y(3))
                send(w_at(first, 160), w_at(first, 160), sib_sem.at[rel], sibling)
            else:
                q = first + 80 * way
                arrived(w_at(q, 80), z_sem.at[way, 4])
                send(w_at(q, 80), w_at(q, 80), y_sem.at[4], at_y(1 if way == 0 else 3))
                send(w_at(q, 80), w_at(q, 80), sib_sem.at[4], sibling)

    def y_poll(rel):
        other = block_rows(rel, c) + (1 - hy) * 160
        arrived(w_at(other, 160), y_sem.at[rel])
        send(w_at(other, 160), w_at(other, 160), sib_sem.at[rel], sibling)

    clip_in.wait()
    conv_in.wait()
    raw = clip_v[...].astype(F32)
    act[:, 0:14, :] = raw / (1.0 + jnp.exp(-raw))
    act[:, 14:16, :] = jnp.zeros((14, 2, 512), F32)
    flat = act[...].reshape(224, 512)
    for k, value in enumerate((pltpu.roll(flat, 1, 0), flat, pltpu.roll(flat, 223, 0))):
        sh[k, 0:16, :] = jnp.zeros((16, 512), BF16)
        sh[k, 240:256, :] = jnp.zeros((16, 512), BF16)
        sh[k, 16:240, :] = value.astype(BF16)
    total = jnp.zeros((224, 128), F32)
    for dy in range(3):
        for dx in range(3):
            taps = jnp.concatenate([conv_v[1, dy, dx]] * 4 + [conv_v[0, dy, dx]] * 4, axis=0)
            total += lax.dot_general(sh[dx, dy * 16 : dy * 16 + 224, :], taps, NT, preferred_element_type=F32)
    cell = lax.broadcasted_iota(jnp.int32, (224, 128), 0)
    lane = lax.broadcasted_iota(jnp.int32, (224, 128), 1)
    parity = ((cell >> 4) & 1) * 2 + (cell & 1)
    spread = jnp.where(((lane >> 4) & 3) == parity, total, 0.0)
    token = lax.broadcasted_iota(jnp.int32, (64, 224), 0)
    cell = lax.broadcasted_iota(jnp.int32, (64, 224), 1)
    mine = (token == (cell >> 5) * 7 + ((cell & 15) >> 1)) & ((cell & 15) < 14)
    both = jnp.dot(
        mine.astype(F32), spread, precision=lax.Precision.HIGHEST, preferred_element_type=F32
    )
    low = lax.broadcasted_iota(jnp.int32, (32, 128), 1) < 64
    this_tap = jnp.where(low, both[0:32], pltpu.roll(both[32:64], 64, 1))
    bsend[...] = jnp.where(low, pltpu.roll(both[0:32], 64, 1), both[32:64])
    send(bsend, brecv, b_sem.at[0], at_x(1))

    w_poll(1)

    gate_in.wait()
    hot = lax.broadcasted_iota(jnp.int32, (16, 35), 1) == step_ref[0]
    gate_row[...] = jnp.dot(hot.astype(F32).astype(BF16), gate_v[...], preferred_element_type=F32)

    arrived(brecv, b_sem.at[0])
    packs[y, zh] = (this_tap + jnp.where(x > 0, brecv[...], 0.0)).astype(BF16)
    send(packs.at[y, zh], packs.at[y, zh], pz_sem.at[0], partner)

    w_poll(2)

    own_heads.wait()
    for d in (1, 2, 3):
        arrived(heads.at[:, pl.ds(d * ROWS, ROWS), :], head_sem.at[d])
        arrived(tail_in.at[d], tail_sem.at[d])
    tail_in[0] = tail_out[:, pl.ds(pl.multiple_of(x * GW, 128), GW)]
    row = lax.broadcasted_iota(jnp.int32, (16, GW), 0)
    ends = [tail_in[j].astype(F32) for j in range(4)]
    for p in range(3):
        value = jnp.zeros((16, GW), F32)
        for j in range(4):
            value = jnp.where(row == j, ends[j][p : p + 1, :], value)
        heads[p, MAIN:ALL, :] = value.astype(BF16)
    key_col = lax.broadcasted_iota(jnp.int32, (ALL, ALL), 1)
    for h in range(HG):
        at = slice(h * HD, (h + 1) * HD)
        scores = lax.dot_general(heads[0, :, at], heads[1, :, at], NT, preferred_element_type=F32)
        scores = jnp.where(key_col < 196, scores * (1.0 / math.sqrt(HD)), -1e30)
        powers = jnp.exp(scores - jnp.max(scores, axis=1, keepdims=True))
        weights = (powers / jnp.sum(powers, axis=1, keepdims=True)).astype(BF16)
        att[:, at] = jnp.dot(weights, heads[2, :, at], preferred_element_type=F32).astype(BF16)

    arrived(packs.at[y, 1 - zh], pz_sem.at[0])
    for d in (1, 3, 2):
        send(packs.at[y], packs.at[y], py_sem.at[4 - d], at_y(d))

    def project(i):
        rel = ORDER[i]
        arrived(w_at(block_rows(rel, 1 - c), CW), sib_sem.at[rel])
        rows = pl.ds(pl.multiple_of(((zl + rel) % 8) * BW, 16), BW)
        value = lax.dot_general(att[...], wg[rows, :], NT, preferred_element_type=F32)
        terms[i] = value[0:MAIN].astype(BF16)
        for j in range(4):
            for t in range(5):
                tsend[j, i * 5 + t : i * 5 + t + 1, :] = value[MAIN + j : MAIN + j + 1, t * 128 : (t + 1) * 128]
        for d in (1, 3, 2):
            send(terms.at[i, pl.ds(d * ROWS, ROWS), :], recv.at[4 - d, i], term_sem.at[4 - d, i], at_x(d))

    own_w.wait()
    w_poll(3)
    project(0)
    y_poll(7)
    y_poll(1)
    w_poll(4)
    project(1)
    y_poll(6)
    project(2)
    y_poll(2)
    project(3)
    y_poll(5)
    project(4)
    y_poll(3)
    project(5)
    y_poll(4)
    project(6)
    project(7)
    for d in (1, 3, 2):
        send(tsend.at[d], trecv.at[4 - d], tt_sem.at[4 - d], at_x(d))

    for d in (1, 2, 3):
        arrived(packs.at[(y + d) % 4], py_sem.at[d])
    chosen = jnp.zeros((32, 128), F32)
    for k in range(8):
        chosen = jnp.where(source_ref[0] == k, packs[k % 4, k // 4].astype(F32), chosen)
    patch[0:32, :] = chosen.astype(BF16)
    patch[32:64, :] = pltpu.roll(chosen, 64, 1).astype(BF16)
    embed_in.wait()
    hidden_in.wait()
    flag = reset_ref[0].astype(F32)
    patches = patch[:, 0:64]

    for i in range(NB):
        at = cols(ORDER[i])
        projected = terms[i, 0:ROWS, :].astype(F32)
        for d in (1, 3, 2):
            arrived(recv.at[d, i], term_sem.at[d, i])
            projected += recv[d, i].astype(F32)
        condition = jnp.dot(patches[0:ROWS], embed_v[:, at], preferred_element_type=F32)
        out_v[0:ROWS, at] = (
            hidden_v[0:ROWS, at].astype(F32) + flag * condition + gate_row[0:1, at] * projected
        ).astype(BF16)
    for d in (1, 2, 3):
        arrived(trecv.at[d], tt_sem.at[d])
    ends = tsend[0] + trecv[1] + trecv[2] + trecv[3]
    for i in range(NB):
        at = cols(ORDER[i])
        projected = jnp.concatenate([ends[i * 5 + t : i * 5 + t + 1, :] for t in range(5)], axis=1)
        condition = jnp.dot(patches[ROWS:64], embed_v[:, at], preferred_element_type=F32)[0:1]
        out_v[ROWS : ROWS + 1, at] = (
            hidden_v[ROWS : ROWS + 1, at].astype(F32) + flag * condition + gate_row[0:1, at] * projected
        ).astype(BF16)
    done = pltpu.make_async_copy(out_v, out_ref, loc_sem.at[len(locals_)])
    done.start()
    for copy in sent:
        copy.wait_send()
    done.wait()


def per_device(qkv, hidden_in, clips, reset, source_group, step_index, conv_weight, embed_weight, out_weight, gate_table):
    anywhere = pl.BlockSpec(memory_space=pl.ANY)
    scalar = pl.BlockSpec(memory_space=pltpu.SMEM)
    dma = pltpu.SemaphoreType.DMA
    result = pl.pallas_call(
        body,
        out_shape=jax.ShapeDtypeStruct((49, D), BF16),
        in_specs=[scalar] * 3 + [anywhere] * 7,
        out_specs=anywhere,
        scratch_shapes=[
            pltpu.VMEM((3, 49, 4 * GW), BF16),
            pltpu.VMEM((49, D), BF16),
            pltpu.VMEM((14, 14, 512), BF16),
            pltpu.VMEM((2, 3, 3, 16, 512), BF16),
            pltpu.VMEM((64, D), BF16),
            pltpu.VMEM((35, D), BF16),
            pltpu.VMEM((49, D), BF16),
            pltpu.VMEM((D, GW), BF16),
            pltpu.VMEM((3, ALL, GW), BF16),
            pltpu.VMEM((16, 4 * GW), BF16),
            pltpu.VMEM((4, 16, GW), BF16),
            pltpu.VMEM((ALL, GW), BF16),
            pltpu.VMEM((NB, MAIN, BW), BF16),
            pltpu.VMEM((4, NB, ROWS, BW), BF16),
            pltpu.VMEM((4, 40, 128), F32),
            pltpu.VMEM((4, 40, 128), F32),
            pltpu.VMEM((14, 16, 512), F32),
            pltpu.VMEM((3, 256, 512), BF16),
            pltpu.VMEM((32, 128), F32),
            pltpu.VMEM((32, 128), F32),
            pltpu.VMEM((4, 2, 32, 128), BF16),
            pltpu.VMEM((16, D), F32),
            pltpu.VMEM((64, 128), BF16),
            dma((9,)),
            dma((96,)),
            dma((4,)),
            dma((4,)),
            dma((2, 5)),
            dma((8,)),
            dma((8,)),
            dma((4, NB)),
            dma((4,)),
            dma((1,)),
            dma((1,)),
            dma((4,)),
        ],
        compiler_params=pltpu.CompilerParams(
            collective_id=0, has_side_effects=True, vmem_limit_bytes=48 * 1024 * 1024
        ),
        cost_estimate=pl.CostEstimate(flops=2_000_000_000, bytes_accessed=8_000_000, transcendentals=400_000),
    )(
        reset,
        source_group,
        step_index,
        qkv[0].transpose(1, 0, 2),
        hidden_in[0],
        clips[0, 0],
        conv_weight.transpose(0, 1, 2, 4, 3),
        embed_weight,
        out_weight.T,
        gate_table,
    )
    return result[None]


def solution(mesh):
    placed = (
        P(("dp", "shard"), "seq", None, None),
        P(("dp", "shard"), "seq", None),
        P(("dp", "shard"), "seq", None, None, None),
        P(("dp", "shard")),
        P(("dp", "shard")),
        P(("dp", "shard")),
        P(),
        P(),
        P("seq", "shard"),
        P(),
    )
    return jax.shard_map(
        per_device,
        mesh=mesh,
        in_specs=placed,
        out_specs=P(("dp", "shard"), "seq", None),
        check_vma=False,
    )
```

```python
import math

import jax
import jax.numpy as jnp
from jax import lax
from jax.experimental import pallas as pl
from jax.experimental.pallas import tpu as pltpu
from jax.sharding import PartitionSpec as P

MESH = pl.DeviceIdType.MESH
BF16, F32 = jnp.bfloat16, jnp.float32
HD = 128
HG = 5
GW = HG * HD
D = 5120
NB = 8
BW = D // NB
CW = BW // 2
ROWS = 48
MAIN = 4 * ROWS
ALL = MAIN + 16
QR = CW // 4
QR0 = 48
CROSSING = 4
HALVES = ((0, 384), (384, 256))
NT = (((1,), (1,)), ((), ()))


def body(
    reset_ref, source_ref, step_ref, qkv_ref, hidden_ref, clip_ref, conv_ref, embed_ref, w_ref, gate_ref,
    out_ref,
    qkv_v, hidden_v, clip_v, conv_v, embed_v, gate_v, out_v,
    wg, heads, tail_out, tail_in, att, terms, cross, recv, tsend, trecv, act, sh, bsend, brecv, packs, midway, gate_row, patch,
    loc_sem, out_sem, w_out_sem, z_sem, y_sem, sib_sem, term_sem, cross_sem, in_sem,
):
    g, s, x = lax.axis_index("dp"), lax.axis_index("shard"), lax.axis_index("seq")
    zh, y, zl, c = g // 4, g % 4, s // 2, s % 2
    z = zh * 8 + zl

    def at_x(d):
        return {"seq": (x + d) % 4}

    def at_y(d):
        return {"dp": zh * 4 + (y + d) % 4}

    def at_z(d):
        zz = (z + d) % 16
        return {"dp": (zz // 8) * 4 + y, "shard": (zz % 8) * 2 + c}

    sibling = {"shard": zl * 2 + 1 - c}

    barrier = pltpu.get_barrier_semaphore()

    def greet(dev):
        pl.semaphore_signal(barrier, inc=1, device_id=dev, device_id_type=MESH)

    for dev in (at_x(1), at_x(2), at_x(3), at_y(1), at_y(2), at_y(3), sibling):
        greet(dev)
    pl.when(z < 15)(lambda: greet(at_z(1)))
    pl.when(z > 0)(lambda: greet(at_z(15)))

    locals_ = []

    def load(src, dst):
        copy = pltpu.make_async_copy(src, dst, loc_sem.at[len(locals_)])
        copy.start()
        locals_.append(copy)
        return copy

    def remote(src, dst, out, sem, dev):
        return pltpu.make_async_remote_copy(
            src_ref=src, dst_ref=dst, send_sem=out, recv_sem=sem, device_id=dev, device_id_type=MESH
        )

    def send(src, dst, out, sem, dev, when=None):
        if when is None:
            remote(src, dst, out, sem, dev).start()
        else:
            pl.when(when)(lambda: remote(src, dst, out, sem, dev).start())

    def arrived(dst, sem):
        remote(dst, dst, out_sem.at[0], sem, sibling).wait_recv()

    ends_of_w = []

    def left(src, out):
        remote(src, src, out, in_sem.at[0], sibling).wait_send()

    near = [-1, 1, -2, 2, -3, 3, 4]
    runs = {0: [1, 2, 3, 4, 5, 6, 7], 1: [-1, 1, 2, 3, 4, 5, 6], 2: [-1, 1, -2, 2, 3, 4, 5]}
    block = [zl]
    for i in range(7):
        off = jnp.int32(near[i])
        for at, run in runs.items():
            off = jnp.where(z == at, run[i], jnp.where(z == 15 - at, -run[i], off))
        block.append((zl + off + 8) % 8)

    def block_rows(b, core):
        return pl.multiple_of(b * BW + core * CW, 16)

    def cols(i):
        return pl.ds(pl.multiple_of(block[i] * BW, 128), BW)

    def w_at(start, size):
        return wg.at[pl.ds(pl.multiple_of(start, 16), size), :]

    qkv_in = load(qkv_ref, qkv_v)
    own_heads = load(
        qkv_ref.at[:, pl.ds(0, ROWS), pl.ds(pl.multiple_of(x * GW, 128), GW)], heads.at[:, pl.ds(0, ROWS), :]
    )
    clip_in = load(clip_ref, clip_v)
    conv_in = load(conv_ref, conv_v)
    own_w = load(w_ref, w_at(block_rows(zl, c), CW))
    embed_in = load(embed_ref, embed_v)
    gate_in = load(gate_ref, gate_v)
    hidden_in = load(hidden_ref, hidden_v)

    pl.semaphore_wait(barrier, 7 + jnp.where(z < 15, 1, 0) + jnp.where(z > 0, 1, 0))

    for d in (1, 3, 2):
        send(
            qkv_ref.at[:, pl.ds(0, ROWS), pl.ds(pl.multiple_of(((x + d) % 4) * GW, 128), GW)],
            heads.at[:, pl.ds((4 - d) * ROWS, ROWS), :],
            out_sem.at[0],
            in_sem.at[0],
            at_x(d),
        )
    quarter = pl.ds(pl.multiple_of(y * QR, 16), QR)
    for way in (0, 1):
        here = (z < 15) if way == 0 else (z > 0)
        send(
            w_ref.at[quarter, :],
            w_at(block_rows(zl, c) + y * QR, QR),
            w_out_sem.at[way],
            z_sem.at[way, 1],
            at_z(1 if way == 0 else 15),
            here,
        )
        ends_of_w.append((QR, w_out_sem.at[way], here))
    send(w_ref, w_at(block_rows(zl, c), CW), out_sem.at[1], sib_sem.at[zl], sibling)

    qkv_in.wait()
    row16 = lax.broadcasted_iota(jnp.int32, (16, 4 * GW), 0)
    tails = [qkv_v[p, ROWS : ROWS + 1, :].astype(F32) for p in range(3)]
    tail_out[...] = jnp.where(
        row16 == 0, tails[0], jnp.where(row16 == 1, tails[1], jnp.where(row16 == 2, tails[2], 0.0))
    ).astype(BF16)
    for d in (1, 3, 2):
        send(
            tail_out.at[:, pl.ds(pl.multiple_of(((x + d) % 4) * GW, 128), GW)],
            tail_in.at[pl.ds((4 - d) * 16, 16), :],
            out_sem.at[0],
            in_sem.at[1],
            at_x(d),
        )

    def comes(u, k):
        if k <= 3:
            return u >= k, None
        if k == 4:
            return u >= 12, (u >= 4) & (u < 12)
        return u >= 8 + k, None

    def w_step(k):
        todo = []
        for way in (0, 1):
            u = z if way == 0 else 15 - z
            b = (z + (8 - k if way == 0 else k)) % 8
            first = block_rows(b, c) + y * QR
            narrow = (0, QR0) if way == 0 else (QR0, QR - QR0)
            out = 2 * k + way if k <= 4 else 5 + k
            on = 13 + 2 * (k - 1) + way if k < 4 else 15 + k
            for full, here in zip((True, False), comes(u, k)):
                if here is None:
                    continue
                lo, size = (0, QR) if full else narrow
                piece = w_at(first + lo, size)
                pl.when(here)(lambda: arrived(piece, z_sem.at[way, k]))
                if full and k < 7:
                    for wide, then in zip((True, False), comes(u + 1, k + 1)):
                        if then is None:
                            continue
                        lo2, size2 = (0, QR) if wide else narrow
                        part = w_at(first + lo2, size2)
                        also = here & then & (u < 15)
                        send(part, part, w_out_sem.at[on], z_sem.at[way, k + 1], at_z(1 if way == 0 else 15), also)
                        ends_of_w.append((size2, w_out_sem.at[on], also))
                todo.append((piece, w_out_sem.at[out], b, here))
                ends_of_w.append((3 * size, w_out_sem.at[out], here))
        for piece, out, b, here in todo:
            for d in (1, 3, 2):
                send(piece, piece, out, y_sem.at[b], at_y(d), here)

    def y_all(i):
        b = block[i]
        arrived(w_at(0, 3 * QR), y_sem.at[b])
        piece = w_at(block_rows(b, c), CW)
        send(piece, piece, out_sem.at[1], sib_sem.at[b], sibling)

    clip_in.wait()
    conv_in.wait()
    raw = clip_v[...].astype(F32)
    act[:, 0:14, :] = raw / (1.0 + jnp.exp(-raw))
    act[:, 14:16, :] = jnp.zeros((14, 2, 512), F32)
    flat = act[...].reshape(224, 512)
    for k, value in enumerate((pltpu.roll(flat, 1, 0), flat, pltpu.roll(flat, 223, 0))):
        sh[k, 0:16, :] = jnp.zeros((16, 512), BF16)
        sh[k, 240:256, :] = jnp.zeros((16, 512), BF16)
        sh[k, 16:240, :] = value.astype(BF16)
    total = jnp.zeros((224, 128), F32)
    for dy in range(3):
        for dx in range(3):
            taps = jnp.concatenate([conv_v[1, dy, dx]] * 4 + [conv_v[0, dy, dx]] * 4, axis=0)
            total += lax.dot_general(sh[dx, dy * 16 : dy * 16 + 224, :], taps, NT, preferred_element_type=F32)
    cell = lax.broadcasted_iota(jnp.int32, (224, 128), 0)
    lane = lax.broadcasted_iota(jnp.int32, (224, 128), 1)
    parity = ((cell >> 4) & 1) * 2 + (cell & 1)
    spread = jnp.where(((lane >> 4) & 3) == parity, total, 0.0)
    token = lax.broadcasted_iota(jnp.int32, (64, 224), 0)
    cell = lax.broadcasted_iota(jnp.int32, (64, 224), 1)
    mine = (token == (cell >> 5) * 7 + ((cell & 15) >> 1)) & ((cell & 15) < 14)
    both = jnp.dot(
        mine.astype(F32), spread, precision=lax.Precision.HIGHEST, preferred_element_type=F32
    )
    low = lax.broadcasted_iota(jnp.int32, (32, 128), 1) < 64
    this_tap = jnp.where(low, both[0:32], pltpu.roll(both[32:64], 64, 1))
    bsend[...] = jnp.where(low, pltpu.roll(both[0:32], 64, 1), both[32:64])
    send(bsend, brecv, out_sem.at[2], in_sem.at[2], at_x(1))

    w_step(1)
    gate_in.wait()
    hot = lax.broadcasted_iota(jnp.int32, (16, 35), 1) == step_ref[0]
    gate_row[...] = jnp.dot(hot.astype(F32).astype(BF16), gate_v[...], preferred_element_type=F32)
    w_step(2)
    y_all(1)
    w_step(3)

    own_heads.wait()
    arrived(heads.at[:, pl.ds(ROWS, 3 * ROWS), :], in_sem.at[0])
    arrived(tail_in.at[pl.ds(16, 48), :], in_sem.at[1])
    tail_in[0:16, :] = tail_out[:, pl.ds(pl.multiple_of(x * GW, 128), GW)]
    row = lax.broadcasted_iota(jnp.int32, (16, GW), 0)
    ends = [tail_in[j * 16 : j * 16 + 16, :].astype(F32) for j in range(4)]
    for p in range(3):
        value = jnp.zeros((16, GW), F32)
        for j in range(4):
            value = jnp.where(row == j, ends[j][p : p + 1, :], value)
        heads[p, MAIN:ALL, :] = value.astype(BF16)
    key_col = lax.broadcasted_iota(jnp.int32, (ALL, ALL), 1)
    for h in range(HG):
        at = slice(h * HD, (h + 1) * HD)
        scores = lax.dot_general(heads[0, :, at], heads[1, :, at], NT, preferred_element_type=F32)
        scores = jnp.where(key_col < 196, scores * (1.0 / math.sqrt(HD)), -1e30)
        powers = jnp.exp(scores - jnp.max(scores, axis=1, keepdims=True))
        weights = (powers / jnp.sum(powers, axis=1, keepdims=True)).astype(BF16)
        att[:, at] = jnp.dot(weights, heads[2, :, at], preferred_element_type=F32).astype(BF16)

    def project(i):
        arrived(w_at(block_rows(block[i], 1 - c), CW), sib_sem.at[block[i]])
        rows = pl.ds(pl.multiple_of(block[i] * BW, 16), BW)
        value = lax.dot_general(att[...], wg[rows, :], NT, preferred_element_type=F32)
        terms[i] = value[0:MAIN].astype(BF16)
        for j in range(4):
            for t in range(5):
                tsend[j, i * 5 + t : i * 5 + t + 1, :] = value[MAIN + j : MAIN + j + 1, t * 128 : (t + 1) * 128]
        if i >= CROSSING:
            for d in (1, 3, 2):
                send(terms.at[i, pl.ds(d * ROWS, ROWS), :], recv.at[4 - d, i], out_sem.at[3], term_sem.at[i], at_x(d))
            return
        for way, (lo, size) in enumerate(HALVES):
            send(
                terms.at[i, pl.ds(2 * ROWS, ROWS), pl.ds(lo, size)],
                cross.at[i, :, pl.ds(lo, size)],
                out_sem.at[3],
                cross_sem.at[i],
                at_x(1 if way == 0 else 3),
            )

    def add_on(i):
        arrived(cross.at[i], cross_sem.at[i])
        for way, (lo, size) in enumerate(HALVES):
            d = 1 if way == 0 else 3
            mine = terms[i, d * ROWS : (d + 1) * ROWS, lo : lo + size].astype(F32)
            terms[i, d * ROWS : (d + 1) * ROWS, lo : lo + size] = (
                mine + cross[i, :, lo : lo + size].astype(F32)
            ).astype(BF16)
            send(terms.at[i, pl.ds(d * ROWS, ROWS), :], recv.at[4 - d, i], out_sem.at[3], term_sem.at[i], at_x(d))

    def pass_frame():
        arrived(brecv, in_sem.at[2])
        packs[y, zh] = (this_tap + jnp.where(x > 0, brecv[...], 0.0)).astype(BF16)
        for way, here in ((0, z < 8), (1, z >= 8)):
            send(packs.at[y, way], midway.at[way], out_sem.at[4], in_sem.at[3 + way], at_z(4 if way == 0 else 12), here)

    def pass_far():
        here = (z >= 4) & (z < 12)
        for way in (0, 1):
            pl.when(here)(lambda: arrived(midway.at[way], in_sem.at[3 + way]))
            send(midway.at[way], packs.at[y, way], out_sem.at[5], in_sem.at[5], at_z(4 if way == 0 else 12), here)

    def pass_patches():
        arrived(packs.at[y, 1 - zh], in_sem.at[5])
        for d in (1, 3, 2):
            send(packs.at[y], packs.at[y], out_sem.at[6], in_sem.at[6], at_y(d))

    def finish(i, patches, flag):
        at = cols(i)
        peers = (1, 3) if i < CROSSING else (1, 2, 3)
        arrived(recv.at[pl.ds(0, len(peers)), i], term_sem.at[i])
        projected = terms[i, 0:ROWS, :].astype(F32)
        for d in peers:
            projected += recv[d, i].astype(F32)
        condition = jnp.dot(patches[0:ROWS], embed_v[:, at], preferred_element_type=F32)
        out_v[0:ROWS, at] = (
            hidden_v[0:ROWS, at].astype(F32) + flag * condition + gate_row[0:1, at] * projected
        ).astype(BF16)

    own_w.wait()
    project(0)
    w_step(4)
    y_all(2)
    pass_frame()
    project(1)
    project(2)
    y_all(3)
    add_on(0)
    w_step(5)
    project(3)
    add_on(1)
    y_all(4)
    add_on(2)
    w_step(6)
    project(4)
    pass_far()
    add_on(3)
    y_all(5)
    w_step(7)
    project(5)
    y_all(6)
    project(6)
    pass_patches()
    y_all(7)
    project(7)
    for d in (1, 3, 2):
        send(tsend.at[d], trecv.at[4 - d], out_sem.at[7], in_sem.at[7], at_x(d))

    arrived(packs.at[pl.ds(0, 3)], in_sem.at[6])
    chosen = jnp.zeros((32, 128), F32)
    for k in range(8):
        chosen = jnp.where(source_ref[0] == k, packs[k % 4, k // 4].astype(F32), chosen)
    patch[0:32, :] = chosen.astype(BF16)
    patch[32:64, :] = pltpu.roll(chosen, 64, 1).astype(BF16)
    embed_in.wait()
    hidden_in.wait()
    flag = reset_ref[0].astype(F32)
    patches = patch[:, 0:64]

    for i in range(NB):
        finish(i, patches, flag)
    arrived(trecv.at[pl.ds(1, 3)], in_sem.at[7])
    ends = tsend[0] + trecv[1] + trecv[2] + trecv[3]
    for i in range(NB):
        at = cols(i)
        projected = jnp.concatenate([ends[i * 5 + t : i * 5 + t + 1, :] for t in range(5)], axis=1)
        condition = jnp.dot(patches[ROWS:64], embed_v[:, at], preferred_element_type=F32)[0:1]
        out_v[ROWS : ROWS + 1, at] = (
            hidden_v[ROWS : ROWS + 1, at].astype(F32) + flag * condition + gate_row[0:1, at] * projected
        ).astype(BF16)
    done = pltpu.make_async_copy(out_v, out_ref, loc_sem.at[len(locals_)])
    done.start()
    left(w_at(0, 9 * ROWS + 3 * 16), out_sem.at[0])
    left(w_at(0, 8 * CW), out_sem.at[1])
    left(bsend, out_sem.at[2])
    left(w_at(0, NB * 3 * ROWS), out_sem.at[3])
    left(packs.at[y, zh], out_sem.at[4])
    pl.when((z >= 4) & (z < 12))(lambda: left(midway, out_sem.at[5]))
    left(packs.at[pl.ds(0, 3)], out_sem.at[6])
    left(trecv.at[pl.ds(1, 3)], out_sem.at[7])
    for size, out, here in ends_of_w:
        pl.when(here)(lambda: left(w_at(0, size), out))
    done.wait()


def per_device(qkv, hidden_in, clips, reset, source_group, step_index, conv_weight, embed_weight, out_weight, gate_table):
    anywhere = pl.BlockSpec(memory_space=pl.ANY)
    scalar = pl.BlockSpec(memory_space=pltpu.SMEM)
    dma = pltpu.SemaphoreType.DMA
    result = pl.pallas_call(
        body,
        out_shape=jax.ShapeDtypeStruct((49, D), BF16),
        in_specs=[scalar] * 3 + [anywhere] * 7,
        out_specs=anywhere,
        scratch_shapes=[
            pltpu.VMEM((3, 49, 4 * GW), BF16),
            pltpu.VMEM((49, D), BF16),
            pltpu.VMEM((14, 14, 512), BF16),
            pltpu.VMEM((2, 3, 3, 16, 512), BF16),
            pltpu.VMEM((64, D), BF16),
            pltpu.VMEM((35, D), BF16),
            pltpu.VMEM((49, D), BF16),
            pltpu.VMEM((D, GW), BF16),
            pltpu.VMEM((3, ALL, GW), BF16),
            pltpu.VMEM((16, 4 * GW), BF16),
            pltpu.VMEM((64, GW), BF16),
            pltpu.VMEM((ALL, GW), BF16),
            pltpu.VMEM((NB, MAIN, BW), BF16),
            pltpu.VMEM((NB, ROWS, BW), BF16),
            pltpu.VMEM((4, NB, ROWS, BW), BF16),
            pltpu.VMEM((4, 40, 128), F32),
            pltpu.VMEM((4, 40, 128), F32),
            pltpu.VMEM((14, 16, 512), F32),
            pltpu.VMEM((3, 256, 512), BF16),
            pltpu.VMEM((32, 128), F32),
            pltpu.VMEM((32, 128), F32),
            pltpu.VMEM((4, 2, 32, 128), BF16),
            pltpu.VMEM((2, 32, 128), BF16),
            pltpu.VMEM((16, D), F32),
            pltpu.VMEM((64, 128), BF16),
            dma((9,)),
            dma((8,)),
            dma((22,)),
            dma((2, 8)),
            dma((8,)),
            dma((8,)),
            dma((NB,)),
            dma((CROSSING,)),
            dma((8,)),
        ],
        compiler_params=pltpu.CompilerParams(
            collective_id=0, has_side_effects=True, vmem_limit_bytes=63 * 1024 * 1024
        ),
        cost_estimate=pl.CostEstimate(flops=2_000_000_000, bytes_accessed=8_000_000, transcendentals=400_000),
    )(
        reset,
        source_group,
        step_index,
        qkv[0].transpose(1, 0, 2),
        hidden_in[0],
        clips[0, 0],
        conv_weight.transpose(0, 1, 2, 4, 3),
        embed_weight,
        out_weight.T,
        gate_table,
    )
    return result[None]


def solution(mesh):
    placed = (
        P(("dp", "shard"), "seq", None, None),
        P(("dp", "shard"), "seq", None),
        P(("dp", "shard"), "seq", None, None, None),
        P(("dp", "shard")),
        P(("dp", "shard")),
        P(("dp", "shard")),
        P(),
        P(),
        P("seq", "shard"),
        P(),
    )
    return jax.shard_map(
        per_device,
        mesh=mesh,
        in_specs=placed,
        out_specs=P(("dp", "shard"), "seq", None),
        check_vma=False,
    )
```

```python
import math

import jax
import jax.numpy as jnp
from jax import lax
from jax.experimental import pallas as pl
from jax.experimental.pallas import tpu as pltpu
from jax.sharding import PartitionSpec as P

MESH = pl.DeviceIdType.MESH
BF16, F32 = jnp.bfloat16, jnp.float32
HD = 128
HG = 5
GW = HG * HD
D = 5120
NB = 8
BW = D // NB
CW = BW // 2
ROWS = 48
MAIN = 4 * ROWS
ALL = MAIN + 16
QR = CW // 4
CROSSING = 7
HALVES = ((0, 384), (384, 256))
NT = (((1,), (1,)), ((), ()))


def body(
    reset_ref, source_ref, step_ref, qkv_ref, hidden_ref, clip_ref, conv_ref, embed_ref, w_ref, gate_ref,
    out_ref,
    qkv_v, hidden_v, clip_v, conv_v, embed_v, gate_v, out_v,
    wg, heads, tail_rows, tail_out, tail_in, att, terms, cross, recv, tsend, tail_terms, trecv, tail_sum, act, sh, bsend, brecv, packs, midway, gate_row, patch,
    loc_sem, out_sem, z_sem, y_sem, sib_sem, term_sem, cross_sem, in_sem,
):
    g, s, x = lax.axis_index("dp"), lax.axis_index("shard"), lax.axis_index("seq")
    zh, y, zl, c = g // 4, g % 4, s // 2, s % 2
    z = zh * 8 + zl

    def at_x(d):
        return {"seq": (x + d) % 4}

    def at_y(d):
        return {"dp": zh * 4 + (y + d) % 4}

    def at_z(d):
        zz = (z + d) % 16
        return {"dp": (zz // 8) * 4 + y, "shard": (zz % 8) * 2 + c}

    sibling = {"shard": zl * 2 + 1 - c}

    barrier = pltpu.get_barrier_semaphore()

    def greet(dev):
        pl.semaphore_signal(barrier, inc=1, device_id=dev, device_id_type=MESH)

    for dev in (at_x(1), at_x(2), at_x(3), at_y(1), at_y(2), at_y(3), sibling):
        greet(dev)
    greet(at_z(15))
    pl.when(z < 15)(lambda: greet(at_z(1)))

    locals_ = []

    def load(src, dst):
        copy = pltpu.make_async_copy(src, dst, loc_sem.at[len(locals_)])
        copy.start()
        locals_.append(copy)
        return copy

    def remote(src, dst, out, sem, dev):
        return pltpu.make_async_remote_copy(
            src_ref=src, dst_ref=dst, send_sem=out, recv_sem=sem, device_id=dev, device_id_type=MESH
        )

    def send(src, dst, out, sem, dev, when=None):
        if when is None:
            remote(src, dst, out, sem, dev).start()
        else:
            pl.when(when)(lambda: remote(src, dst, out, sem, dev).start())

    def arrived(dst, sem):
        remote(dst, dst, out_sem.at[0], sem, sibling).wait_recv()

    def left(src, out):
        remote(src, src, out, in_sem.at[0], sibling).wait_send()

    near = [-1, 1, -2, 2, -3, 3, 4]
    runs = {0: [1, 2, -1, 3, -2, -3, 4], 1: [-1, 1, 2, -2, 3, -3, 4], 2: [-1, 1, -2, 2, 3, -3, 4]}
    block = [zl]
    for i in range(7):
        off = jnp.int32(near[i])
        for at, run in runs.items():
            off = jnp.where(z == at, run[i], jnp.where(z == 15 - at, -run[i], off))
        block.append((zl + off + 8) % 8)

    def block_rows(b, core):
        return pl.multiple_of(b * BW + core * CW, 16)

    def cols(i):
        return pl.ds(pl.multiple_of(block[i] * BW, 128), BW)

    def w_at(start, size):
        return wg.at[pl.ds(pl.multiple_of(start, 16), size), :]

    qkv_in = load(qkv_ref, qkv_v)
    own_heads = load(
        qkv_ref.at[:, pl.ds(0, ROWS), pl.ds(pl.multiple_of(x * GW, 128), GW)], heads.at[:, pl.ds(0, ROWS), :]
    )
    clip_in = load(clip_ref, clip_v)
    conv_in = load(conv_ref, conv_v)
    own_w = load(w_ref, w_at(block_rows(zl, c), CW))
    embed_in = load(embed_ref, embed_v)
    gate_in = load(gate_ref, gate_v)
    hidden_in = load(hidden_ref, hidden_v)

    qkv_in.wait()
    tail_rows[...] = jnp.zeros_like(tail_rows)
    for p in range(3):
        last = qkv_v[p, ROWS : ROWS + 1, :].astype(F32)
        for t in range(4 * HG):
            at = (t // HG) * 16 + p * HG + t % HG
            tail_rows[at : at + 1, :] = last[:, t * HD : (t + 1) * HD]
    tail_out[...] = tail_rows[...].astype(BF16)
    pl.semaphore_wait(barrier, 8 + jnp.where(z > 0, 1, 0))

    for d in (1, 3, 2):
        send(
            tail_out.at[pl.ds(pl.multiple_of(((x + d) % 4) * 16, 16), 16), :],
            tail_in.at[pl.ds((4 - d) * 16, 16), :],
            out_sem.at[8],
            in_sem.at[1],
            at_x(d),
        )

    for part, (lo, size) in enumerate(HALVES):
        for d in (2, 1, 3):
            send(
                qkv_ref.at[:, pl.ds(0, ROWS), pl.ds(pl.multiple_of(((x + d) % 4) * GW + lo, 128), size)],
                heads.at[:, pl.ds((4 - d) * ROWS, ROWS), pl.ds(lo, size)],
                out_sem.at[0],
                in_sem.at[8 + part],
                at_x(d),
            )
    def own_piece(q, way, when):
        start = ((y + q) % 4) * QR
        send(
            w_ref.at[pl.ds(pl.multiple_of(start, 16), QR), :],
            w_at(block_rows(zl, c) + start, QR),
            out_sem.at[1],
            z_sem.at[way, 2 + q],
            at_z(1 if way == 0 else 15),
            when,
        )

    for q in (0, 1):
        own_piece(q, 0, None)
        own_piece(q, 1, z > 0)
    send(w_ref, w_at(block_rows(zl, c), CW), out_sem.at[1], sib_sem.at[zl], sibling)

    def w_piece(k, q, way):
        b = (z + (8 - k if way == 0 else k)) % 8
        return w_at(block_rows(b, c) + ((y + q) % 4) * QR, QR), b

    def pass_on(k, q, way, when):
        piece, _ = w_piece(k, q, way)
        send(piece, piece, out_sem.at[1], z_sem.at[way, 2 * k + 2 + q], at_z(1 if way == 0 else 15), when)

    def w_step(k, q, late):
        todo = []
        for way in (0, 1):
            if k == 4 and q != way:
                continue
            crosses = (z if way == 0 else 15 - z) < k
            here = crosses if late else jnp.logical_not(crosses)
            piece, b = w_piece(k, q, way)
            pl.when(here)(lambda: arrived(piece, z_sem.at[way, 2 * k + q]))
            if k < 3 or (k == 3 and q == way):
                pass_on(k, q, way, here & (z > 0) if way == 1 and k < 3 and not late else here)
            todo.append((piece, b, here))
        for piece, b, here in todo:
            send(piece, piece, out_sem.at[1], y_sem.at[q, b], at_y(1 if q == 0 else 3), here)
            send(piece, piece, out_sem.at[1], sib_sem.at[b], sibling, here)

    def w_back():
        for q in (0, 1):
            own_piece(q, 1, z == 0)
        for k in (1, 2):
            for q in (0, 1):
                pass_on(k, q, 1, z == 0)

    def y_near(i):
        for q, d in ((0, 3), (1, 2)):
            piece = w_at(block_rows(block[i], c) + ((y + d) % 4) * QR, QR)
            arrived(piece, y_sem.at[q, block[i]])
            send(piece, piece, out_sem.at[1], sib_sem.at[block[i]], sibling)

    clip_in.wait()
    conv_in.wait()
    raw = clip_v[...].astype(F32)
    act[:, 0:14, :] = raw / (1.0 + jnp.exp(-raw))
    act[:, 14:16, :] = jnp.zeros((14, 2, 512), F32)
    flat = act[...].reshape(224, 512)
    for k, value in enumerate((pltpu.roll(flat, 1, 0), flat, pltpu.roll(flat, 223, 0))):
        sh[k, 0:16, :] = jnp.zeros((16, 512), BF16)
        sh[k, 240:256, :] = jnp.zeros((16, 512), BF16)
        sh[k, 16:240, :] = value.astype(BF16)
    total = jnp.zeros((224, 128), F32)
    for dy in range(3):
        for dx in range(3):
            taps = jnp.concatenate([conv_v[1, dy, dx]] * 4 + [conv_v[0, dy, dx]] * 4, axis=0)
            total += lax.dot_general(sh[dx, dy * 16 : dy * 16 + 224, :], taps, NT, preferred_element_type=F32)
    cell = lax.broadcasted_iota(jnp.int32, (224, 128), 0)
    lane = lax.broadcasted_iota(jnp.int32, (224, 128), 1)
    parity = ((cell >> 4) & 1) * 2 + (cell & 1)
    spread = jnp.where(((lane >> 4) & 3) == parity, total, 0.0)
    token = lax.broadcasted_iota(jnp.int32, (64, 224), 0)
    cell = lax.broadcasted_iota(jnp.int32, (64, 224), 1)
    mine = (token == (cell >> 5) * 7 + ((cell & 15) >> 1)) & ((cell & 15) < 14)
    both = jnp.dot(
        mine.astype(F32), spread, precision=lax.Precision.HIGHEST, preferred_element_type=F32
    )
    low = lax.broadcasted_iota(jnp.int32, (32, 128), 1) < 64
    this_tap = jnp.where(low, both[0:32], pltpu.roll(both[32:64], 64, 1))
    bsend[...] = jnp.where(low, pltpu.roll(both[0:32], 64, 1), both[32:64])
    send(bsend, brecv, out_sem.at[2], in_sem.at[2], at_x(1))

    w_step(1, 0, False)
    gate_in.wait()
    hot = lax.broadcasted_iota(jnp.int32, (16, 35), 1) == step_ref[0]
    gate_row[...] = jnp.dot(hot.astype(F32).astype(BF16), gate_v[...], preferred_element_type=F32)

    own_heads.wait()
    arrived(tail_in.at[pl.ds(16, 48), :], in_sem.at[1])
    tail_in[0:16, :] = tail_out[pl.ds(pl.multiple_of(x * 16, 16), 16), :]
    tail_rows[...] = tail_in[...].astype(F32)
    row = lax.broadcasted_iota(jnp.int32, (16, HD), 0)
    for p in range(3):
        for t in range(HG):
            value = jnp.zeros((16, HD), F32)
            for j in range(4):
                at = j * 16 + p * HG + t
                value = jnp.where(row == j, tail_rows[at : at + 1, :], value)
            heads[p, MAIN:ALL, t * HD : (t + 1) * HD] = value.astype(BF16)
    key_col = lax.broadcasted_iota(jnp.int32, (ALL, ALL), 1)

    def attend(part):
        lo, size = HALVES[part]
        arrived(heads.at[:, pl.ds(ROWS, 3 * ROWS), pl.ds(lo, size)], in_sem.at[8 + part])
        for h in range(lo // HD, (lo + size) // HD):
            at = slice(h * HD, (h + 1) * HD)
            scores = lax.dot_general(heads[0, :, at], heads[1, :, at], NT, preferred_element_type=F32)
            scores = jnp.where(key_col < 196, scores * (1.0 / math.sqrt(HD)), -1e30)
            powers = jnp.exp(scores - jnp.max(scores, axis=1, keepdims=True))
            weights = (powers / jnp.sum(powers, axis=1, keepdims=True)).astype(BF16)
            att[:, at] = jnp.dot(weights, heads[2, :, at], preferred_element_type=F32).astype(BF16)

    tsend[:, 40:48, :] = jnp.zeros((4, 8, 128), F32)

    def halves(i):
        return HALVES if i % 2 == 0 else HALVES[::-1]

    def project(i):
        arrived(w_at(block_rows(block[i], 1 - c), CW), sib_sem.at[block[i]])
        rows = pl.ds(pl.multiple_of(block[i] * BW, 16), BW)
        value = lax.dot_general(att[...], wg[rows, :], NT, preferred_element_type=F32)
        terms[i] = value[0:MAIN].astype(BF16)
        for j in range(4):
            for t in range(5):
                tsend[j, i * 5 + t : i * 5 + t + 1, :] = value[MAIN + j : MAIN + j + 1, t * 128 : (t + 1) * 128]
        if i >= CROSSING:
            for d in (1, 3, 2):
                send(terms.at[i, pl.ds(d * ROWS, ROWS), :], recv.at[4 - d, i], out_sem.at[3], term_sem.at[i], at_x(d))
            return
        for way, (lo, size) in enumerate(halves(i)):
            send(
                terms.at[i, pl.ds(2 * ROWS, ROWS), pl.ds(lo, size)],
                cross.at[i, :, pl.ds(lo, size)],
                out_sem.at[3],
                cross_sem.at[i],
                at_x(1 if way == 0 else 3),
            )

    def add_on(i):
        arrived(cross.at[i], cross_sem.at[i])
        for way, (lo, size) in enumerate(halves(i)):
            d = 1 if way == 0 else 3
            mine = terms[i, d * ROWS : (d + 1) * ROWS, lo : lo + size].astype(F32)
            terms[i, d * ROWS : (d + 1) * ROWS, lo : lo + size] = (
                mine + cross[i, :, lo : lo + size].astype(F32)
            ).astype(BF16)
            send(terms.at[i, pl.ds(d * ROWS, ROWS), :], recv.at[4 - d, i], out_sem.at[3], term_sem.at[i], at_x(d))

    def pass_frame():
        arrived(brecv, in_sem.at[2])
        packs[y, zh] = (this_tap + jnp.where(x > 0, brecv[...], 0.0)).astype(BF16)
        for way, here in ((0, z < 8), (1, z >= 8)):
            send(packs.at[y, way], midway.at[way], out_sem.at[4], in_sem.at[3 + way], at_z(4 if way == 0 else 12), here)

    def pass_far():
        here = (z >= 4) & (z < 12)
        for way in (0, 1):
            pl.when(here)(lambda: arrived(midway.at[way], in_sem.at[3 + way]))
            send(midway.at[way], packs.at[y, way], out_sem.at[5], in_sem.at[5], at_z(4 if way == 0 else 12), here)

    def pass_patches():
        arrived(packs.at[y, 1 - zh], in_sem.at[5])
        for d in (1, 3, 2):
            send(packs.at[y], packs.at[y], out_sem.at[6], in_sem.at[6], at_y(d))

    def choose_patches():
        arrived(packs.at[pl.ds(0, 3)], in_sem.at[6])
        chosen = jnp.zeros((32, 128), F32)
        for k in range(8):
            chosen = jnp.where(source_ref[0] == k, packs[k % 4, k // 4].astype(F32), chosen)
        patch[0:32, :] = chosen.astype(BF16)
        patch[32:64, :] = pltpu.roll(chosen, 64, 1).astype(BF16)

    outs = []

    def finish(i):
        at = cols(i)
        peers = (1, 3) if i < CROSSING else (1, 2, 3)
        arrived(recv.at[pl.ds(0, len(peers)), i], term_sem.at[i])
        projected = terms[i, 0:ROWS, :].astype(F32)
        for d in peers:
            projected += recv[d, i].astype(F32)
        last = jnp.concatenate([tail_sum[i * 5 + t : i * 5 + t + 1, :] for t in range(5)], axis=1)
        projected = jnp.concatenate([projected, last], axis=0)
        condition = jnp.dot(patch[:, 0:64], embed_v[:, at], preferred_element_type=F32)[0 : ROWS + 1]
        out_v[i] = (
            hidden_v[:, at].astype(F32) + reset_ref[0].astype(F32) * condition + gate_row[0:1, at] * projected
        ).astype(BF16)
        copy = pltpu.make_async_copy(out_v.at[i], out_ref.at[:, at], loc_sem.at[len(locals_) + i])
        copy.start()
        outs.append(copy)

    def send_tails(lo, size, k):
        tail_terms[:, lo : lo + size, :] = tsend[:, lo : lo + size, :].astype(BF16)
        for d in (1, 3, 2):
            send(
                tail_terms.at[d, pl.ds(lo, size), :],
                trecv.at[4 - d, pl.ds(lo, size), :],
                out_sem.at[7],
                in_sem.at[k],
                at_x(d),
            )

    def sum_tails(lo, size, k):
        arrived(trecv.at[pl.ds(1, 3), pl.ds(lo, size), :], in_sem.at[k])
        value = tsend[0, lo : lo + size, :]
        for d in (1, 2, 3):
            value += trecv[d, lo : lo + size, :].astype(F32)
        tail_sum[lo : lo + size, :] = value

    w_step(1, 1, False)
    attend(0)
    w_step(2, 0, False)
    y_near(1)
    w_step(2, 1, False)
    w_step(1, 0, True)
    w_back()
    attend(1)
    own_w.wait()
    project(0)
    w_step(3, 0, False)
    pass_frame()
    w_step(1, 1, True)
    y_near(2)
    project(1)
    w_step(3, 1, False)
    w_step(2, 0, True)
    y_near(3)
    w_step(2, 1, True)
    project(2)
    add_on(0)
    y_near(4)
    w_step(3, 0, True)
    project(3)
    add_on(1)
    w_step(4, 0, False)
    w_step(4, 1, False)
    w_step(3, 1, True)
    y_near(5)
    project(4)
    add_on(2)
    pass_far()
    w_step(4, 0, True)
    w_step(4, 1, True)
    y_near(6)
    project(5)
    add_on(3)
    y_near(7)
    project(6)
    send_tails(0, 32, 7)
    add_on(4)
    pass_patches()
    project(7)
    add_on(5)
    send_tails(32, 16, 10)
    add_on(6)
    choose_patches()
    embed_in.wait()
    hidden_in.wait()
    sum_tails(0, 32, 7)
    finish(0)
    finish(1)
    finish(2)
    finish(3)
    finish(4)
    finish(5)
    sum_tails(32, 16, 10)
    finish(6)
    finish(7)
    left(w_at(0, 9 * ROWS), out_sem.at[0])
    left(w_at(0, CW + 56 * QR), out_sem.at[1])
    left(bsend, out_sem.at[2])
    left(w_at(0, NB * 3 * ROWS), out_sem.at[3])
    left(packs.at[y, zh], out_sem.at[4])
    pl.when((z >= 4) & (z < 12))(lambda: left(midway, out_sem.at[5]))
    left(packs.at[pl.ds(0, 3)], out_sem.at[6])
    left(trecv.at[pl.ds(1, 3)], out_sem.at[7])
    left(tail_in.at[pl.ds(16, 48), :], out_sem.at[8])
    for copy in outs:
        copy.wait()


def per_device(qkv, hidden_in, clips, reset, source_group, step_index, conv_weight, embed_weight, out_weight, gate_table):
    anywhere = pl.BlockSpec(memory_space=pl.ANY)
    scalar = pl.BlockSpec(memory_space=pltpu.SMEM)
    dma = pltpu.SemaphoreType.DMA
    result = pl.pallas_call(
        body,
        out_shape=jax.ShapeDtypeStruct((49, D), BF16),
        in_specs=[scalar] * 3 + [anywhere] * 7,
        out_specs=anywhere,
        scratch_shapes=[
            pltpu.VMEM((3, 49, 4 * GW), BF16),
            pltpu.VMEM((49, D), BF16),
            pltpu.VMEM((14, 14, 512), BF16),
            pltpu.VMEM((2, 3, 3, 16, 512), BF16),
            pltpu.VMEM((64, D), BF16),
            pltpu.VMEM((35, D), BF16),
            pltpu.VMEM((NB, 49, BW), BF16),
            pltpu.VMEM((D, GW), BF16),
            pltpu.VMEM((3, ALL, GW), BF16),
            pltpu.VMEM((64, HD), F32),
            pltpu.VMEM((64, HD), BF16),
            pltpu.VMEM((64, HD), BF16),
            pltpu.VMEM((ALL, GW), BF16),
            pltpu.VMEM((NB, MAIN, BW), BF16),
            pltpu.VMEM((NB, ROWS, BW), BF16),
            pltpu.VMEM((4, NB, ROWS, BW), BF16),
            pltpu.VMEM((4, 48, 128), F32),
            pltpu.VMEM((4, 48, 128), BF16),
            pltpu.VMEM((4, 48, 128), BF16),
            pltpu.VMEM((48, 128), F32),
            pltpu.VMEM((14, 16, 512), F32),
            pltpu.VMEM((3, 256, 512), BF16),
            pltpu.VMEM((32, 128), F32),
            pltpu.VMEM((32, 128), F32),
            pltpu.VMEM((4, 2, 32, 128), BF16),
            pltpu.VMEM((2, 32, 128), BF16),
            pltpu.VMEM((16, D), F32),
            pltpu.VMEM((64, 128), BF16),
            dma((16,)),
            dma((9,)),
            dma((2, 10)),
            dma((2, 8)),
            dma((8,)),
            dma((NB,)),
            dma((CROSSING,)),
            dma((11,)),
        ],
        compiler_params=pltpu.CompilerParams(
            collective_id=0, has_side_effects=True, vmem_limit_bytes=63 * 1024 * 1024
        ),
        cost_estimate=pl.CostEstimate(flops=2_000_000_000, bytes_accessed=8_000_000, transcendentals=400_000),
    )(
        reset,
        source_group,
        step_index,
        qkv[0].transpose(1, 0, 2),
        hidden_in[0],
        clips[0, 0],
        conv_weight.transpose(0, 1, 2, 4, 3),
        embed_weight,
        out_weight.T,
        gate_table,
    )
    return result[None]


def solution(mesh):
    placed = (
        P(("dp", "shard"), "seq", None, None),
        P(("dp", "shard"), "seq", None),
        P(("dp", "shard"), "seq", None, None, None),
        P(("dp", "shard")),
        P(("dp", "shard")),
        P(("dp", "shard")),
        P(),
        P(),
        P("seq", "shard"),
        P(),
    )
    return jax.shard_map(
        per_device,
        mesh=mesh,
        in_specs=placed,
        out_specs=P(("dp", "shard"), "seq", None),
        check_vma=False,
    )
```

```python
import math

import jax
import jax.numpy as jnp
from jax import lax
from jax.experimental import pallas as pl
from jax.experimental.pallas import tpu as pltpu
from jax.sharding import PartitionSpec as P

MESH = pl.DeviceIdType.MESH
BF16, F32 = jnp.bfloat16, jnp.float32
HD = 128
HG = 5
GW = HG * HD
D = 5120
NB = 8
BW = D // NB
CW = BW // 2
ROWS = 48
MAIN = 4 * ROWS
ALL = MAIN + 16
QR = CW // 4
CROSSING = (3, 4, 5, 6)
HALVES = ((0, 384), (384, 256))
NT = (((1,), (1,)), ((), ()))


def body(
    scalars, qkv_ref, hidden_ref, clip_ref, conv_ref, embed_ref, w_ref, gate_ref,
    out_ref,
    qkv_v, hidden_v, clip_v, conv_v, embed_v, gate_v, out_v,
    wg, heads, tail_rows, tail_out, tail_in, att, terms, cross, recv, tsend, tail_terms, trecv, tail_sum, act, sh, bsend, brecv, packs, midway, gate_row, patch,
    loc_sem, out_sem, z_sem, y_sem, sib_sem, term_sem, cross_sem, in_sem,
):
    g, s, x = lax.axis_index("dp"), lax.axis_index("shard"), lax.axis_index("seq")
    zh, y, zl, c = g // 4, g % 4, s // 2, s % 2
    z = zh * 8 + zl

    def at_x(d):
        return {"seq": (x + d) % 4}

    def at_y(d):
        return {"dp": zh * 4 + (y + d) % 4}

    def at_z(d):
        zz = (z + d) % 16
        return {"dp": (zz // 8) * 4 + y, "shard": (zz % 8) * 2 + c}

    sibling = {"shard": zl * 2 + 1 - c}

    barrier = pltpu.get_barrier_semaphore()

    def greet(dev):
        pl.semaphore_signal(barrier, inc=1, device_id=dev, device_id_type=MESH)

    for dev in (at_x(1), at_x(2), at_x(3), at_y(1), at_y(2), at_y(3), sibling):
        greet(dev)
    greet(at_z(15))
    pl.when(z < 15)(lambda: greet(at_z(1)))

    locals_ = []

    def load(src, dst):
        copy = pltpu.make_async_copy(src, dst, loc_sem.at[len(locals_)])
        copy.start()
        locals_.append(copy)
        return copy

    def remote(src, dst, out, sem, dev):
        return pltpu.make_async_remote_copy(
            src_ref=src, dst_ref=dst, send_sem=out, recv_sem=sem, device_id=dev, device_id_type=MESH
        )

    def send(src, dst, out, sem, dev, when=None):
        if when is None:
            remote(src, dst, out, sem, dev).start()
        else:
            pl.when(when)(lambda: remote(src, dst, out, sem, dev).start())

    def arrived(dst, sem):
        remote(dst, dst, out_sem.at[0], sem, sibling).wait_recv()

    def left(src, out):
        remote(src, src, out, in_sem.at[0], sibling).wait_send()

    near = [-1, 1, -2, 2, -3, 3, 4]
    runs = {0: [1, 2, -1, 3, -2, -3, 4], 1: [-1, 1, 2, -2, 3, -3, 4], 2: [-1, 1, -2, 2, 3, -3, 4]}
    block = [zl]
    for i in range(7):
        off = jnp.int32(near[i])
        for at, run in runs.items():
            off = jnp.where(z == at, run[i], jnp.where(z == 15 - at, -run[i], off))
        block.append((zl + off + 8) % 8)

    def block_rows(b, core):
        return pl.multiple_of(b * BW + core * CW, 16)

    def cols(i):
        return pl.ds(pl.multiple_of(block[i] * BW, 128), BW)

    def w_at(start, size):
        return wg.at[pl.ds(pl.multiple_of(start, 16), size), :]

    qkv_in = load(qkv_ref, qkv_v)
    own_heads = load(
        qkv_ref.at[:, pl.ds(0, ROWS), pl.ds(pl.multiple_of(x * GW, 128), GW)], heads.at[:, pl.ds(0, ROWS), :]
    )
    clip_in = load(clip_ref, clip_v)
    conv_in = load(conv_ref, conv_v)
    own_w = load(w_ref, w_at(block_rows(zl, c), CW))
    embed_in = load(embed_ref, embed_v)
    gate_in = load(gate_ref, gate_v)
    hidden_in = load(hidden_ref, hidden_v)

    pl.semaphore_wait(barrier, 8 + jnp.where(z > 0, 1, 0))

    def send_heads(part):
        lo, size = HALVES[part]
        for d in (2, 1, 3):
            send(
                qkv_ref.at[:, pl.ds(0, ROWS), pl.ds(pl.multiple_of(((x + d) % 4) * GW + lo, 128), size)],
                heads.at[:, pl.ds((4 - d) * ROWS, ROWS), pl.ds(lo, size)],
                out_sem.at[0],
                in_sem.at[8 + part],
                at_x(d),
            )

    send_heads(0)
    def own_piece(q, way, when):
        start = ((y + q) % 4) * QR
        send(
            w_ref.at[pl.ds(pl.multiple_of(start, 16), QR), :],
            w_at(block_rows(zl, c) + start, QR),
            out_sem.at[1],
            z_sem.at[way, 2 + q],
            at_z(1 if way == 0 else 15),
            when,
        )

    for r in (0, 1):
        own_piece(r, 0, None)
        own_piece(1 - r, 1, z > 0)
    send(w_ref, w_at(block_rows(zl, c), CW), out_sem.at[1], sib_sem.at[zl], sibling)

    qkv_in.wait()
    tail_rows[...] = jnp.zeros_like(tail_rows)
    for p in range(3):
        last = qkv_v[p, ROWS : ROWS + 1, :].astype(F32)
        for t in range(4 * HG):
            at = (t // HG) * 16 + p * HG + t % HG
            tail_rows[at : at + 1, :] = last[:, t * HD : (t + 1) * HD]
    tail_out[...] = tail_rows[...].astype(BF16)
    for d in (2, 1, 3):
        send(
            tail_out.at[pl.ds(pl.multiple_of(((x + d) % 4) * 16, 16), 16), :],
            tail_in.at[pl.ds((4 - d) * 16, 16), :],
            out_sem.at[8],
            in_sem.at[1],
            at_x(d),
        )
    send_heads(1)

    def w_piece(k, q, way):
        b = (z + (8 - k if way == 0 else k)) % 8
        return w_at(block_rows(b, c) + ((y + q) % 4) * QR, QR), b

    def pass_on(k, q, way, when):
        piece, _ = w_piece(k, q, way)
        send(piece, piece, out_sem.at[1], z_sem.at[way, 2 * k + 2 + q], at_z(1 if way == 0 else 15), when)

    def w_step(k, r, late, only=None):
        todo = []
        for way in (0, 1):
            q = way if r == 0 else 1 - way
            crosses = (z if way == 0 else 15 - z) < k
            here = crosses if late else jnp.logical_not(crosses)
            here = here if only is None else here & only
            piece, b = w_piece(k, q, way)
            pl.when(here)(lambda: arrived(piece, z_sem.at[way, 2 * k + q]))
            if k < 3 or (k == 3 and r == 0):
                pass_on(k, q, way, here & (z > 0) if way == 1 and k < 3 and not late else here)
            todo.append((piece, b, q, here))
        for piece, b, q, here in todo:
            send(piece, piece, out_sem.at[1], y_sem.at[q, b], at_y(1 if q == 0 else 3), here)
            send(piece, piece, out_sem.at[1], sib_sem.at[b], sibling, here)

    def w_back():
        for q in (1, 0):
            own_piece(q, 1, z == 0)
        for k in (1, 2):
            for q in (1, 0):
                pass_on(k, q, 1, z == 0)

    def y_near(i):
        for q, d in ((0, 3), (1, 2)):
            piece = w_at(block_rows(block[i], c) + ((y + d) % 4) * QR, QR)
            arrived(piece, y_sem.at[q, block[i]])
            send(piece, piece, out_sem.at[1], sib_sem.at[block[i]], sibling)

    clip_in.wait()
    conv_in.wait()
    raw = clip_v[...].astype(F32)
    act[:, 0:14, :] = raw / (1.0 + jnp.exp(-raw))
    act[:, 14:16, :] = jnp.zeros((14, 2, 512), F32)
    flat = act[...].reshape(224, 512)
    for k, value in enumerate((pltpu.roll(flat, 1, 0), flat, pltpu.roll(flat, 223, 0))):
        sh[k, 0:16, :] = jnp.zeros((16, 512), BF16)
        sh[k, 240:256, :] = jnp.zeros((16, 512), BF16)
        sh[k, 16:240, :] = value.astype(BF16)
    total = jnp.zeros((224, 128), F32)
    for dy in range(3):
        for dx in range(3):
            taps = jnp.concatenate([conv_v[1, dy, dx]] * 4 + [conv_v[0, dy, dx]] * 4, axis=0)
            total += lax.dot_general(sh[dx, dy * 16 : dy * 16 + 224, :], taps, NT, preferred_element_type=F32)
    cell = lax.broadcasted_iota(jnp.int32, (224, 128), 0)
    lane = lax.broadcasted_iota(jnp.int32, (224, 128), 1)
    parity = ((cell >> 4) & 1) * 2 + (cell & 1)
    spread = jnp.where(((lane >> 4) & 3) == parity, total, 0.0)
    token = lax.broadcasted_iota(jnp.int32, (64, 224), 0)
    cell = lax.broadcasted_iota(jnp.int32, (64, 224), 1)
    mine = (token == (cell >> 5) * 7 + ((cell & 15) >> 1)) & ((cell & 15) < 14)
    both = jnp.dot(
        mine.astype(F32), spread, precision=lax.Precision.HIGHEST, preferred_element_type=F32
    )
    low = lax.broadcasted_iota(jnp.int32, (32, 128), 1) < 64
    this_tap = jnp.where(low, both[0:32], pltpu.roll(both[32:64], 64, 1))
    bsend[...] = jnp.where(low, pltpu.roll(both[0:32], 64, 1), both[32:64])
    send(bsend, brecv, out_sem.at[2], in_sem.at[2], at_x(1))

    w_step(1, 0, False)
    w_step(1, 1, False)
    gate_in.wait()
    hot = lax.broadcasted_iota(jnp.int32, (16, 35), 1) == scalars[2]
    gate_row[...] = jnp.dot(hot.astype(F32).astype(BF16), gate_v[...], preferred_element_type=F32)

    w_step(2, 0, False)

    own_heads.wait()
    arrived(tail_in.at[pl.ds(16, 48), :], in_sem.at[1])
    tail_in[0:16, :] = tail_out[pl.ds(pl.multiple_of(x * 16, 16), 16), :]
    tail_rows[...] = tail_in[...].astype(F32)
    row = lax.broadcasted_iota(jnp.int32, (16, HD), 0)
    for p in range(3):
        for t in range(HG):
            value = jnp.zeros((16, HD), F32)
            for j in range(4):
                at = j * 16 + p * HG + t
                value = jnp.where(row == j, tail_rows[at : at + 1, :], value)
            heads[p, MAIN:ALL, t * HD : (t + 1) * HD] = value.astype(BF16)
    key_col = lax.broadcasted_iota(jnp.int32, (ALL, ALL), 1)

    def attend(part):
        lo, size = HALVES[part]
        arrived(heads.at[:, pl.ds(ROWS, 3 * ROWS), pl.ds(lo, size)], in_sem.at[8 + part])
        for h in range(lo // HD, (lo + size) // HD):
            at = slice(h * HD, (h + 1) * HD)
            scores = lax.dot_general(heads[0, :, at], heads[1, :, at], NT, preferred_element_type=F32)
            scores = jnp.where(key_col < 196, scores * (1.0 / math.sqrt(HD)), -1e30)
            powers = jnp.exp(scores - jnp.max(scores, axis=1, keepdims=True))
            weights = (powers / jnp.sum(powers, axis=1, keepdims=True)).astype(BF16)
            att[:, at] = jnp.dot(weights, heads[2, :, at], preferred_element_type=F32).astype(BF16)

    tsend[:, 40:48, :] = jnp.zeros((4, 8, 128), F32)

    def halves(i):
        return HALVES if i % 2 == 0 else HALVES[::-1]

    def project(i):
        arrived(w_at(block_rows(block[i], 1 - c), CW), sib_sem.at[block[i]])
        rows = pl.ds(pl.multiple_of(block[i] * BW, 16), BW)
        value = lax.dot_general(att[...], wg[rows, :], NT, preferred_element_type=F32)
        terms[i] = value[0:MAIN].astype(BF16)
        for j in range(4):
            for t in range(5):
                tsend[j, i * 5 + t : i * 5 + t + 1, :] = value[MAIN + j : MAIN + j + 1, t * 128 : (t + 1) * 128]
        if i not in CROSSING:
            for d in (1, 3, 2):
                send(terms.at[i, pl.ds(d * ROWS, ROWS), :], recv.at[4 - d, i], out_sem.at[3], term_sem.at[i], at_x(d))
            return
        for way, (lo, size) in enumerate(halves(i)):
            send(
                terms.at[i, pl.ds(2 * ROWS, ROWS), pl.ds(lo, size)],
                cross.at[i, :, pl.ds(lo, size)],
                out_sem.at[3],
                cross_sem.at[i],
                at_x(1 if way == 0 else 3),
            )

    def add_on(i):
        arrived(cross.at[i], cross_sem.at[i])
        for way, (lo, size) in enumerate(halves(i)):
            d = 1 if way == 0 else 3
            mine = terms[i, d * ROWS : (d + 1) * ROWS, lo : lo + size].astype(F32)
            terms[i, d * ROWS : (d + 1) * ROWS, lo : lo + size] = (
                mine + cross[i, :, lo : lo + size].astype(F32)
            ).astype(BF16)
            send(terms.at[i, pl.ds(d * ROWS, ROWS), :], recv.at[4 - d, i], out_sem.at[3], term_sem.at[i], at_x(d))

    def pass_frame():
        arrived(brecv, in_sem.at[2])
        packs[y, zh] = (this_tap + jnp.where(x > 0, brecv[...], 0.0)).astype(BF16)
        for way, here in ((0, z < 8), (1, z >= 8)):
            send(packs.at[y, way], midway.at[way], out_sem.at[4], in_sem.at[3 + way], at_z(4 if way == 0 else 12), here)

    def pass_far():
        here = (z >= 4) & (z < 12)
        for way in (0, 1):
            pl.when(here)(lambda: arrived(midway.at[way], in_sem.at[3 + way]))
            send(midway.at[way], packs.at[y, way], out_sem.at[5], in_sem.at[5], at_z(4 if way == 0 else 12), here)

    def pass_patches():
        arrived(packs.at[y, 1 - zh], in_sem.at[5])
        for d in (1, 3, 2):
            send(packs.at[y], packs.at[y], out_sem.at[6], in_sem.at[6], at_y(d))

    def choose_patches():
        arrived(packs.at[pl.ds(0, 3)], in_sem.at[6])
        chosen = jnp.zeros((32, 128), F32)
        for k in range(8):
            chosen = jnp.where(scalars[1] == k, packs[k % 4, k // 4].astype(F32), chosen)
        patch[0:32, :] = chosen.astype(BF16)
        patch[32:64, :] = pltpu.roll(chosen, 64, 1).astype(BF16)

    def finish(i):
        at = cols(i)
        peers = (1, 3) if i in CROSSING else (1, 2, 3)
        arrived(recv.at[pl.ds(0, len(peers)), i], term_sem.at[i])
        projected = terms[i, 0:ROWS, :].astype(F32)
        for d in peers:
            projected += recv[d, i].astype(F32)
        last = jnp.concatenate([tail_sum[i * 5 + t : i * 5 + t + 1, :] for t in range(5)], axis=1)
        projected = jnp.concatenate([projected, last], axis=0)
        condition = jnp.dot(patch[:, 0:64], embed_v[:, at], preferred_element_type=F32)[0 : ROWS + 1]
        out_v[i] = (
            hidden_v[:, at].astype(F32) + scalars[0].astype(F32) * condition + gate_row[0:1, at] * projected
        ).astype(BF16)
        copy = pltpu.make_async_copy(out_v.at[i], out_ref.at[:, at], loc_sem.at[len(locals_)])
        copy.start()

    def send_tails(lo, size, k):
        tail_terms[:, lo : lo + size, :] = tsend[:, lo : lo + size, :].astype(BF16)
        for d in (1, 3, 2):
            send(
                tail_terms.at[d, pl.ds(lo, size), :],
                trecv.at[4 - d, pl.ds(lo, size), :],
                out_sem.at[7],
                in_sem.at[k],
                at_x(d),
            )

    def sum_tails(lo, size, k):
        arrived(trecv.at[pl.ds(1, 3), pl.ds(lo, size), :], in_sem.at[k])
        value = tsend[0, lo : lo + size, :]
        for d in (1, 2, 3):
            value += trecv[d, lo : lo + size, :].astype(F32)
        tail_sum[lo : lo + size, :] = value

    attend(0)
    y_near(1)
    w_step(2, 1, False)
    w_step(1, 0, True)
    w_back()
    attend(1)
    own_w.wait()
    edge = jnp.minimum(z, 15 - z)
    project(0)
    w_step(3, 0, False)
    pass_frame()
    w_step(1, 1, True)
    y_near(2)
    w_step(2, 0, True, z != 0)
    project(1)
    w_step(3, 1, False)
    w_step(2, 0, True, z == 0)
    w_step(2, 1, True)
    y_near(3)
    w_step(3, 0, True, edge >= 2)
    project(2)
    w_step(4, 0, False)
    w_step(3, 0, True, edge < 2)
    y_near(4)
    w_step(3, 1, True, edge >= 2)
    project(3)
    w_step(3, 1, True, edge < 2)
    y_near(5)
    w_step(4, 0, True, edge >= 2)
    project(4)
    w_step(4, 0, True, edge < 2)
    pass_far()
    add_on(3)
    y_near(6)
    project(5)
    add_on(4)
    y_near(7)
    project(6)
    add_on(5)
    send_tails(0, 32, 7)
    project(7)
    send_tails(32, 16, 10)
    add_on(6)
    pass_patches()
    choose_patches()
    embed_in.wait()
    hidden_in.wait()
    sum_tails(0, 32, 7)
    finish(0)
    finish(1)
    finish(2)
    finish(3)
    finish(4)
    finish(5)
    sum_tails(32, 16, 10)
    finish(6)
    finish(7)
    left(w_at(0, 9 * ROWS), out_sem.at[0])
    left(w_at(0, CW + 56 * QR), out_sem.at[1])
    left(bsend, out_sem.at[2])
    left(w_at(0, NB * 3 * ROWS), out_sem.at[3])
    left(packs.at[y, zh], out_sem.at[4])
    pl.when((z >= 4) & (z < 12))(lambda: left(midway, out_sem.at[5]))
    left(packs.at[pl.ds(0, 3)], out_sem.at[6])
    left(trecv.at[pl.ds(1, 3)], out_sem.at[7])
    left(tail_in.at[pl.ds(16, 48), :], out_sem.at[8])
    pltpu.make_async_copy(out_v, out_v, loc_sem.at[len(locals_)]).wait()


def per_device(qkv, hidden_in, clips, reset, source_group, step_index, conv_weight, embed_weight, out_weight, gate_table):
    anywhere = pl.BlockSpec(memory_space=pl.ANY)
    dma = pltpu.SemaphoreType.DMA
    result = pl.pallas_call(
        body,
        out_shape=jax.ShapeDtypeStruct((49, D), BF16),
        in_specs=[pl.BlockSpec(memory_space=pltpu.SMEM)] + [anywhere] * 7,
        out_specs=anywhere,
        scratch_shapes=[
            pltpu.VMEM((3, 49, 4 * GW), BF16),
            pltpu.VMEM((49, D), BF16),
            pltpu.VMEM((14, 14, 512), BF16),
            pltpu.VMEM((2, 3, 3, 16, 512), BF16),
            pltpu.VMEM((64, D), BF16),
            pltpu.VMEM((35, D), BF16),
            pltpu.VMEM((NB, 49, BW), BF16),
            pltpu.VMEM((D, GW), BF16),
            pltpu.VMEM((3, ALL, GW), BF16),
            pltpu.VMEM((64, HD), F32),
            pltpu.VMEM((64, HD), BF16),
            pltpu.VMEM((64, HD), BF16),
            pltpu.VMEM((ALL, GW), BF16),
            pltpu.VMEM((NB, MAIN, BW), BF16),
            pltpu.VMEM((NB, ROWS, BW), BF16),
            pltpu.VMEM((4, NB, ROWS, BW), BF16),
            pltpu.VMEM((4, 48, 128), F32),
            pltpu.VMEM((4, 48, 128), BF16),
            pltpu.VMEM((4, 48, 128), BF16),
            pltpu.VMEM((48, 128), F32),
            pltpu.VMEM((14, 16, 512), F32),
            pltpu.VMEM((3, 256, 512), BF16),
            pltpu.VMEM((32, 128), F32),
            pltpu.VMEM((32, 128), F32),
            pltpu.VMEM((4, 2, 32, 128), BF16),
            pltpu.VMEM((2, 32, 128), BF16),
            pltpu.VMEM((16, D), F32),
            pltpu.VMEM((64, 128), BF16),
            dma((9,)),
            dma((9,)),
            dma((2, 10)),
            dma((2, 8)),
            dma((8,)),
            dma((NB,)),
            dma((NB,)),
            dma((11,)),
        ],
        compiler_params=pltpu.CompilerParams(
            collective_id=0, has_side_effects=True, vmem_limit_bytes=48 * 1024 * 1024
        ),
        cost_estimate=pl.CostEstimate(flops=2_000_000_000, bytes_accessed=8_000_000, transcendentals=400_000),
    )(
        jnp.concatenate([reset, source_group, step_index]),
        *(
            pltpu.with_memory_space_constraint(operand, pltpu.HBM)
            for operand in (
                qkv[0].transpose(1, 0, 2),
                hidden_in[0],
                clips[0, 0],
                conv_weight.transpose(0, 1, 2, 4, 3),
                embed_weight,
                out_weight.T,
                gate_table,
            )
        )
    )
    return result[None]


def solution(mesh):
    placed = (
        P(("dp", "shard"), "seq", None, None),
        P(("dp", "shard"), "seq", None),
        P(("dp", "shard"), "seq", None, None, None),
        P(("dp", "shard")),
        P(("dp", "shard")),
        P(("dp", "shard")),
        P(),
        P(),
        P("seq", "shard"),
        P(),
    )
    return jax.shard_map(
        per_device,
        mesh=mesh,
        in_specs=placed,
        out_specs=P(("dp", "shard"), "seq", None),
        check_vma=False,
    )
```

```python
import math

import jax
import jax.numpy as jnp
from jax import lax
from jax.experimental import pallas as pl
from jax.experimental.pallas import tpu as pltpu
from jax.sharding import PartitionSpec as P

MESH = pl.DeviceIdType.MESH
BF16, F32 = jnp.bfloat16, jnp.float32
HD = 128
HG = 5
GW = HG * HD
D = 5120
NB = 8
BW = D // NB
CW = BW // 2
ROWS = 48
MAIN = 4 * ROWS
ALL = MAIN + 16
QR = CW // 4
CROSSING = (3, 4, 5, 6)
HALVES = ((0, 384), (384, 256))
NT = (((1,), (1,)), ((), ()))


def body(
    reset_ref, source_ref, step_ref, qkv_ref, hidden_ref, clip_ref, conv_ref, embed_ref, w_ref, gate_ref,
    out_ref,
    qkv_v, hidden_v, clip_v, conv_v, embed_v, gate_v, out_v,
    wg, heads, tail_rows, tail_out, tail_in, att, terms, cross, recv, tsend, tail_terms, trecv, tail_sum, act, sh, bsend, brecv, packs, midway, gate_row, patch,
    loc_sem, out_sem, z_sem, y_sem, sib_sem, term_sem, cross_sem, in_sem,
):
    g, s, x = lax.axis_index("dp"), lax.axis_index("shard"), lax.axis_index("seq")
    zh, y, zl, c = g // 4, g % 4, s // 2, s % 2
    z = zh * 8 + zl

    def at_x(d):
        return {"seq": (x + d) % 4}

    def at_y(d):
        return {"dp": zh * 4 + (y + d) % 4}

    def at_z(d):
        zz = (z + d) % 16
        return {"dp": (zz // 8) * 4 + y, "shard": (zz % 8) * 2 + c}

    sibling = {"shard": zl * 2 + 1 - c}

    barrier = pltpu.get_barrier_semaphore()

    def greet(dev):
        pl.semaphore_signal(barrier, inc=1, device_id=dev, device_id_type=MESH)

    for dev in (at_x(1), at_x(2), at_x(3), at_y(1), at_y(2), at_y(3), sibling):
        greet(dev)
    greet(at_z(15))
    pl.when(z < 15)(lambda: greet(at_z(1)))

    locals_ = []

    def load(src, dst):
        copy = pltpu.make_async_copy(src, dst, loc_sem.at[len(locals_)])
        copy.start()
        locals_.append(copy)
        return copy

    def remote(src, dst, out, sem, dev):
        return pltpu.make_async_remote_copy(
            src_ref=src, dst_ref=dst, send_sem=out, recv_sem=sem, device_id=dev, device_id_type=MESH
        )

    def send(src, dst, out, sem, dev, when=None):
        if when is None:
            remote(src, dst, out, sem, dev).start()
        else:
            pl.when(when)(lambda: remote(src, dst, out, sem, dev).start())

    def arrived(dst, sem):
        remote(dst, dst, out_sem.at[0], sem, sibling).wait_recv()

    def left(src, out):
        remote(src, src, out, in_sem.at[0], sibling).wait_send()

    near = [-1, 1, -2, 2, -3, 3, 4]
    runs = {0: [1, 2, -1, 3, -2, -3, 4], 1: [-1, 1, 2, -2, 3, -3, 4], 2: [-1, 1, -2, 2, 3, -3, 4]}
    block = [zl]
    for i in range(7):
        off = jnp.int32(near[i])
        for at, run in runs.items():
            off = jnp.where(z == at, run[i], jnp.where(z == 15 - at, -run[i], off))
        block.append((zl + off + 8) % 8)

    def block_rows(b, core):
        return pl.multiple_of(b * BW + core * CW, 16)

    def cols(i):
        return pl.ds(pl.multiple_of(block[i] * BW, 128), BW)

    def w_at(start, size):
        return wg.at[pl.ds(pl.multiple_of(start, 16), size), :]

    qkv_in = load(qkv_ref, qkv_v)
    own_heads = load(
        qkv_ref.at[:, pl.ds(0, ROWS), pl.ds(pl.multiple_of(x * GW, 128), GW)], heads.at[:, pl.ds(0, ROWS), :]
    )
    clip_in = load(clip_ref, clip_v)
    conv_in = load(conv_ref, conv_v)
    own_w = load(w_ref, w_at(block_rows(zl, c), CW))
    embed_in = load(embed_ref, embed_v)
    gate_in = load(gate_ref, gate_v)
    hidden_in = load(hidden_ref, hidden_v)

    pl.semaphore_wait(barrier, 8 + jnp.where(z > 0, 1, 0))

    def send_heads(part):
        lo, size = HALVES[part]
        for d in (2, 1, 3):
            send(
                qkv_ref.at[:, pl.ds(0, ROWS), pl.ds(pl.multiple_of(((x + d) % 4) * GW + lo, 128), size)],
                heads.at[:, pl.ds((4 - d) * ROWS, ROWS), pl.ds(lo, size)],
                out_sem.at[0],
                in_sem.at[8 + part],
                at_x(d),
            )

    send_heads(0)
    def own_piece(q, way, when):
        start = ((y + q) % 4) * QR
        send(
            w_ref.at[pl.ds(pl.multiple_of(start, 16), QR), :],
            w_at(block_rows(zl, c) + start, QR),
            out_sem.at[1],
            z_sem.at[way, 2 + q],
            at_z(1 if way == 0 else 15),
            when,
        )

    for r in (0, 1):
        own_piece(r, 0, None)
        own_piece(1 - r, 1, z > 0)
    send(w_ref, w_at(block_rows(zl, c), CW), out_sem.at[1], sib_sem.at[zl], sibling)

    qkv_in.wait()
    tail_rows[...] = jnp.zeros_like(tail_rows)
    for p in range(3):
        last = qkv_v[p, ROWS : ROWS + 1, :].astype(F32)
        for t in range(4 * HG):
            at = (t // HG) * 16 + p * HG + t % HG
            tail_rows[at : at + 1, :] = last[:, t * HD : (t + 1) * HD]
    tail_out[...] = tail_rows[...].astype(BF16)
    for d in (2, 1, 3):
        send(
            tail_out.at[pl.ds(pl.multiple_of(((x + d) % 4) * 16, 16), 16), :],
            tail_in.at[pl.ds((4 - d) * 16, 16), :],
            out_sem.at[8],
            in_sem.at[1],
            at_x(d),
        )
    send_heads(1)

    def w_piece(k, q, way):
        b = (z + (8 - k if way == 0 else k)) % 8
        return w_at(block_rows(b, c) + ((y + q) % 4) * QR, QR), b

    def pass_on(k, q, way, when):
        piece, _ = w_piece(k, q, way)
        send(piece, piece, out_sem.at[1], z_sem.at[way, 2 * k + 2 + q], at_z(1 if way == 0 else 15), when)

    def w_step(k, r, late, only=None):
        todo = []
        for way in (0, 1):
            q = way if r == 0 else 1 - way
            crosses = (z if way == 0 else 15 - z) < k
            here = crosses if late else jnp.logical_not(crosses)
            here = here if only is None else here & only
            piece, b = w_piece(k, q, way)
            pl.when(here)(lambda: arrived(piece, z_sem.at[way, 2 * k + q]))
            if k < 3 or (k == 3 and r == 0):
                pass_on(k, q, way, here & (z > 0) if way == 1 and k < 3 and not late else here)
            todo.append((piece, b, q, here))
        for piece, b, q, here in todo:
            send(piece, piece, out_sem.at[1], y_sem.at[q, b], at_y(1 if q == 0 else 3), here)
            send(piece, piece, out_sem.at[1], sib_sem.at[b], sibling, here)

    def w_back():
        for q in (1, 0):
            own_piece(q, 1, z == 0)
        for k in (1, 2):
            for q in (1, 0):
                pass_on(k, q, 1, z == 0)

    def y_near(i):
        for q, d in ((0, 3), (1, 2)):
            piece = w_at(block_rows(block[i], c) + ((y + d) % 4) * QR, QR)
            arrived(piece, y_sem.at[q, block[i]])
            send(piece, piece, out_sem.at[1], sib_sem.at[block[i]], sibling)

    clip_in.wait()
    conv_in.wait()
    raw = clip_v[...].astype(F32)
    act[:, 0:14, :] = raw / (1.0 + jnp.exp(-raw))
    act[:, 14:16, :] = jnp.zeros((14, 2, 512), F32)
    flat = act[...].reshape(224, 512)
    for k, value in enumerate((pltpu.roll(flat, 1, 0), flat, pltpu.roll(flat, 223, 0))):
        sh[k, 0:16, :] = jnp.zeros((16, 512), BF16)
        sh[k, 240:256, :] = jnp.zeros((16, 512), BF16)
        sh[k, 16:240, :] = value.astype(BF16)
    total = jnp.zeros((224, 128), F32)
    for dy in range(3):
        for dx in range(3):
            taps = jnp.concatenate([conv_v[1, dy, dx]] * 4 + [conv_v[0, dy, dx]] * 4, axis=0)
            total += lax.dot_general(sh[dx, dy * 16 : dy * 16 + 224, :], taps, NT, preferred_element_type=F32)
    cell = lax.broadcasted_iota(jnp.int32, (224, 128), 0)
    lane = lax.broadcasted_iota(jnp.int32, (224, 128), 1)
    parity = ((cell >> 4) & 1) * 2 + (cell & 1)
    spread = jnp.where(((lane >> 4) & 3) == parity, total, 0.0)
    token = lax.broadcasted_iota(jnp.int32, (64, 224), 0)
    cell = lax.broadcasted_iota(jnp.int32, (64, 224), 1)
    mine = (token == (cell >> 5) * 7 + ((cell & 15) >> 1)) & ((cell & 15) < 14)
    both = jnp.dot(
        mine.astype(F32), spread, precision=lax.Precision.HIGHEST, preferred_element_type=F32
    )
    low = lax.broadcasted_iota(jnp.int32, (32, 128), 1) < 64
    this_tap = jnp.where(low, both[0:32], pltpu.roll(both[32:64], 64, 1))
    bsend[...] = jnp.where(low, pltpu.roll(both[0:32], 64, 1), both[32:64])
    send(bsend, brecv, out_sem.at[2], in_sem.at[2], at_x(1))

    w_step(1, 0, False)
    w_step(1, 1, False)
    gate_in.wait()
    hot = lax.broadcasted_iota(jnp.int32, (16, 35), 1) == step_ref[...]
    gate_row[...] = jnp.dot(hot.astype(F32).astype(BF16), gate_v[...], preferred_element_type=F32)

    w_step(2, 0, False)

    own_heads.wait()
    arrived(tail_in.at[pl.ds(16, 48), :], in_sem.at[1])
    tail_in[0:16, :] = tail_out[pl.ds(pl.multiple_of(x * 16, 16), 16), :]
    tail_rows[...] = tail_in[...].astype(F32)
    row = lax.broadcasted_iota(jnp.int32, (16, HD), 0)
    for p in range(3):
        for t in range(HG):
            value = jnp.zeros((16, HD), F32)
            for j in range(4):
                at = j * 16 + p * HG + t
                value = jnp.where(row == j, tail_rows[at : at + 1, :], value)
            heads[p, MAIN:ALL, t * HD : (t + 1) * HD] = value.astype(BF16)
    key_col = lax.broadcasted_iota(jnp.int32, (ALL, ALL), 1)

    def attend(part):
        lo, size = HALVES[part]
        arrived(heads.at[:, pl.ds(ROWS, 3 * ROWS), pl.ds(lo, size)], in_sem.at[8 + part])
        for h in range(lo // HD, (lo + size) // HD):
            at = slice(h * HD, (h + 1) * HD)
            scores = lax.dot_general(heads[0, :, at], heads[1, :, at], NT, preferred_element_type=F32)
            scores = jnp.where(key_col < 196, scores * (1.0 / math.sqrt(HD)), -1e30)
            powers = jnp.exp(scores - jnp.max(scores, axis=1, keepdims=True))
            weights = (powers / jnp.sum(powers, axis=1, keepdims=True)).astype(BF16)
            att[:, at] = jnp.dot(weights, heads[2, :, at], preferred_element_type=F32).astype(BF16)

    tsend[:, 40:48, :] = jnp.zeros((4, 8, 128), F32)

    def halves(i):
        return HALVES if i % 2 == 0 else HALVES[::-1]

    def project(i):
        arrived(w_at(block_rows(block[i], 1 - c), CW), sib_sem.at[block[i]])
        rows = pl.ds(pl.multiple_of(block[i] * BW, 16), BW)
        value = lax.dot_general(att[...], wg[rows, :], NT, preferred_element_type=F32)
        terms[i] = value[0:MAIN].astype(BF16)
        for j in range(4):
            for t in range(5):
                tsend[j, i * 5 + t : i * 5 + t + 1, :] = value[MAIN + j : MAIN + j + 1, t * 128 : (t + 1) * 128]
        if i not in CROSSING:
            for d in (1, 3, 2):
                send(terms.at[i, pl.ds(d * ROWS, ROWS), :], recv.at[4 - d, i], out_sem.at[3], term_sem.at[i], at_x(d))
            return
        for way, (lo, size) in enumerate(halves(i)):
            send(
                terms.at[i, pl.ds(2 * ROWS, ROWS), pl.ds(lo, size)],
                cross.at[i, :, pl.ds(lo, size)],
                out_sem.at[3],
                cross_sem.at[i],
                at_x(1 if way == 0 else 3),
            )

    def add_on(i):
        arrived(cross.at[i], cross_sem.at[i])
        for way, (lo, size) in enumerate(halves(i)):
            d = 1 if way == 0 else 3
            mine = terms[i, d * ROWS : (d + 1) * ROWS, lo : lo + size].astype(F32)
            terms[i, d * ROWS : (d + 1) * ROWS, lo : lo + size] = (
                mine + cross[i, :, lo : lo + size].astype(F32)
            ).astype(BF16)
            send(terms.at[i, pl.ds(d * ROWS, ROWS), :], recv.at[4 - d, i], out_sem.at[3], term_sem.at[i], at_x(d))

    def pass_frame():
        arrived(brecv, in_sem.at[2])
        packs[y, zh] = (this_tap + jnp.where(x > 0, brecv[...], 0.0)).astype(BF16)
        for way, here in ((0, z < 8), (1, z >= 8)):
            send(packs.at[y, way], midway.at[way], out_sem.at[4], in_sem.at[3 + way], at_z(4 if way == 0 else 12), here)

    def pass_far():
        here = (z >= 4) & (z < 12)
        for way in (0, 1):
            pl.when(here)(lambda: arrived(midway.at[way], in_sem.at[3 + way]))
            send(midway.at[way], packs.at[y, way], out_sem.at[5], in_sem.at[5], at_z(4 if way == 0 else 12), here)

    def pass_patches():
        arrived(packs.at[y, 1 - zh], in_sem.at[5])
        for d in (1, 3, 2):
            send(packs.at[y], packs.at[y], out_sem.at[6], in_sem.at[6], at_y(d))

    def choose_patches():
        arrived(packs.at[pl.ds(0, 3)], in_sem.at[6])
        chosen = jnp.zeros((32, 128), F32)
        for k in range(8):
            chosen = jnp.where(source_ref[...] == k, packs[k % 4, k // 4].astype(F32), chosen)
        patch[0:32, :] = chosen.astype(BF16)
        patch[32:64, :] = pltpu.roll(chosen, 64, 1).astype(BF16)

    def finish(i):
        at = cols(i)
        peers = (1, 3) if i in CROSSING else (1, 2, 3)
        arrived(recv.at[pl.ds(0, len(peers)), i], term_sem.at[i])
        projected = terms[i, 0:ROWS, :].astype(F32)
        for d in peers:
            projected += recv[d, i].astype(F32)
        last = jnp.concatenate([tail_sum[i * 5 + t : i * 5 + t + 1, :] for t in range(5)], axis=1)
        projected = jnp.concatenate([projected, last], axis=0)
        condition = jnp.dot(patch[:, 0:64], embed_v[:, at], preferred_element_type=F32)[0 : ROWS + 1]
        out_v[i] = (
            hidden_v[:, at].astype(F32) + reset_ref[...].astype(F32) * condition + gate_row[0:1, at] * projected
        ).astype(BF16)
        copy = pltpu.make_async_copy(out_v.at[i], out_ref.at[:, at], loc_sem.at[len(locals_)])
        copy.start()

    def send_tails(lo, size, k):
        tail_terms[:, lo : lo + size, :] = tsend[:, lo : lo + size, :].astype(BF16)
        for d in (1, 3, 2):
            send(
                tail_terms.at[d, pl.ds(lo, size), :],
                trecv.at[4 - d, pl.ds(lo, size), :],
                out_sem.at[7],
                in_sem.at[k],
                at_x(d),
            )

    def sum_tails(lo, size, k):
        arrived(trecv.at[pl.ds(1, 3), pl.ds(lo, size), :], in_sem.at[k])
        value = tsend[0, lo : lo + size, :]
        for d in (1, 2, 3):
            value += trecv[d, lo : lo + size, :].astype(F32)
        tail_sum[lo : lo + size, :] = value

    attend(0)
    y_near(1)
    w_step(2, 1, False)
    w_step(1, 0, True)
    w_back()
    attend(1)
    own_w.wait()
    edge = jnp.minimum(z, 15 - z)
    project(0)
    w_step(3, 0, False)
    pass_frame()
    w_step(1, 1, True)
    y_near(2)
    w_step(2, 0, True, z != 0)
    project(1)
    w_step(3, 1, False)
    w_step(2, 0, True, z == 0)
    w_step(2, 1, True)
    y_near(3)
    w_step(3, 0, True, edge >= 2)
    project(2)
    w_step(4, 0, False)
    w_step(3, 0, True, edge < 2)
    y_near(4)
    w_step(3, 1, True, edge >= 2)
    project(3)
    w_step(3, 1, True, edge < 2)
    y_near(5)
    w_step(4, 0, True, edge >= 2)
    project(4)
    w_step(4, 0, True, edge < 2)
    pass_far()
    add_on(3)
    y_near(6)
    project(5)
    add_on(4)
    y_near(7)
    project(6)
    add_on(5)
    send_tails(0, 32, 7)
    project(7)
    send_tails(32, 16, 10)
    add_on(6)
    pass_patches()
    choose_patches()
    embed_in.wait()
    hidden_in.wait()
    sum_tails(0, 32, 7)
    finish(0)
    finish(1)
    finish(2)
    finish(3)
    finish(4)
    finish(5)
    sum_tails(32, 16, 10)
    finish(6)
    finish(7)
    left(w_at(0, 9 * ROWS), out_sem.at[0])
    left(w_at(0, CW + 56 * QR), out_sem.at[1])
    left(bsend, out_sem.at[2])
    left(w_at(0, NB * 3 * ROWS), out_sem.at[3])
    left(packs.at[y, zh], out_sem.at[4])
    pl.when((z >= 4) & (z < 12))(lambda: left(midway, out_sem.at[5]))
    left(packs.at[pl.ds(0, 3)], out_sem.at[6])
    left(trecv.at[pl.ds(1, 3)], out_sem.at[7])
    left(tail_in.at[pl.ds(16, 48), :], out_sem.at[8])
    pltpu.make_async_copy(out_v, out_v, loc_sem.at[len(locals_)]).wait()


def per_device(qkv, hidden_in, clips, reset, source_group, step_index, conv_weight, embed_weight, out_weight, gate_table):
    anywhere = pl.BlockSpec(memory_space=pl.ANY)
    dma = pltpu.SemaphoreType.DMA
    result = pl.pallas_call(
        body,
        out_shape=jax.ShapeDtypeStruct((49, D), BF16),
        in_specs=[pl.BlockSpec(memory_space=pltpu.VMEM)] * 3 + [anywhere] * 7,
        out_specs=anywhere,
        scratch_shapes=[
            pltpu.VMEM((3, 49, 4 * GW), BF16),
            pltpu.VMEM((49, D), BF16),
            pltpu.VMEM((14, 14, 512), BF16),
            pltpu.VMEM((2, 3, 3, 16, 512), BF16),
            pltpu.VMEM((64, D), BF16),
            pltpu.VMEM((35, D), BF16),
            pltpu.VMEM((NB, 49, BW), BF16),
            pltpu.VMEM((D, GW), BF16),
            pltpu.VMEM((3, ALL, GW), BF16),
            pltpu.VMEM((64, HD), F32),
            pltpu.VMEM((64, HD), BF16),
            pltpu.VMEM((64, HD), BF16),
            pltpu.VMEM((ALL, GW), BF16),
            pltpu.VMEM((NB, MAIN, BW), BF16),
            pltpu.VMEM((NB, ROWS, BW), BF16),
            pltpu.VMEM((4, NB, ROWS, BW), BF16),
            pltpu.VMEM((4, 48, 128), F32),
            pltpu.VMEM((4, 48, 128), BF16),
            pltpu.VMEM((4, 48, 128), BF16),
            pltpu.VMEM((48, 128), F32),
            pltpu.VMEM((14, 16, 512), F32),
            pltpu.VMEM((3, 256, 512), BF16),
            pltpu.VMEM((32, 128), F32),
            pltpu.VMEM((32, 128), F32),
            pltpu.VMEM((4, 2, 32, 128), BF16),
            pltpu.VMEM((2, 32, 128), BF16),
            pltpu.VMEM((16, D), F32),
            pltpu.VMEM((64, 128), BF16),
            dma((9,)),
            dma((9,)),
            dma((2, 10)),
            dma((2, 8)),
            dma((8,)),
            dma((NB,)),
            dma((NB,)),
            dma((11,)),
        ],
        compiler_params=pltpu.CompilerParams(
            collective_id=0, has_side_effects=True, vmem_limit_bytes=48 * 1024 * 1024
        ),
        cost_estimate=pl.CostEstimate(flops=2_000_000_000, bytes_accessed=8_000_000, transcendentals=400_000),
    )(
        reset.reshape(1, 1),
        source_group.reshape(1, 1),
        step_index.reshape(1, 1),
        *(
            pltpu.with_memory_space_constraint(operand, pltpu.HBM)
            for operand in (
                qkv[0].transpose(1, 0, 2),
                hidden_in[0],
                clips[0, 0],
                conv_weight.transpose(0, 1, 2, 4, 3),
                embed_weight,
                out_weight.T,
                gate_table,
            )
        )
    )
    return result[None]


def solution(mesh):
    placed = (
        P(("dp", "shard"), "seq", None, None),
        P(("dp", "shard"), "seq", None),
        P(("dp", "shard"), "seq", None, None, None),
        P(("dp", "shard")),
        P(("dp", "shard")),
        P(("dp", "shard")),
        P(),
        P(),
        P("seq", "shard"),
        P(),
    )
    return jax.shard_map(
        per_device,
        mesh=mesh,
        in_specs=placed,
        out_specs=P(("dp", "shard"), "seq", None),
        check_vma=False,
    )
```

```python
import math

import jax
import jax.numpy as jnp
from jax import lax
from jax.experimental import pallas as pl
from jax.experimental.pallas import tpu as pltpu
from jax.sharding import PartitionSpec as P

MESH = pl.DeviceIdType.MESH
BF16, F32 = jnp.bfloat16, jnp.float32
HD = 128
HG = 5
GW = HG * HD
D = 5120
NB = 8
BW = D // NB
CW = BW // 2
ROWS = 48
MAIN = 4 * ROWS
ALL = MAIN + 16
QR = CW // 4
CROSSING = (3, 4, 5, 6)
HALVES = ((0, 384), (384, 256))
NT = (((1,), (1,)), ((), ()))


def body(
    reset_ref, source_ref, step_ref, qkv_ref, hidden_ref, clip_ref, conv_ref, embed_ref, w_ref, gate_ref,
    out_ref,
    qkv_v, hidden_v, clip_v, conv_v, embed_v, gate_v, out_v,
    wg, heads, tail_rows, tail_out, tail_in, att, terms, cross, recv, tsend, tail_terms, trecv, tail_sum, act, sh, bsend, brecv, packs, midway, gate_row, patch,
    loc_sem, out_sem, z_sem, y_sem, sib_sem, term_sem, cross_sem, in_sem,
):
    g, s, x = lax.axis_index("dp"), lax.axis_index("shard"), lax.axis_index("seq")
    zh, y, zl, c = g // 4, g % 4, s // 2, s % 2
    z = zh * 8 + zl

    def at_x(d):
        return {"seq": (x + d) % 4}

    def at_y(d):
        return {"dp": zh * 4 + (y + d) % 4}

    def at_z(d):
        zz = (z + d) % 16
        return {"dp": (zz // 8) * 4 + y, "shard": (zz % 8) * 2 + c}

    sibling = {"shard": zl * 2 + 1 - c}

    barrier = pltpu.get_barrier_semaphore()

    def greet(dev):
        pl.semaphore_signal(barrier, inc=1, device_id=dev, device_id_type=MESH)

    for dev in (at_x(1), at_x(2), at_x(3), at_y(1), at_y(2), at_y(3), sibling):
        greet(dev)
    greet(at_z(15))
    pl.when(z < 15)(lambda: greet(at_z(1)))

    locals_ = []

    def load(src, dst):
        copy = pltpu.make_async_copy(src, dst, loc_sem.at[len(locals_)])
        copy.start()
        locals_.append(copy)
        return copy

    def remote(src, dst, out, sem, dev):
        return pltpu.make_async_remote_copy(
            src_ref=src, dst_ref=dst, send_sem=out, recv_sem=sem, device_id=dev, device_id_type=MESH
        )

    def send(src, dst, out, sem, dev, when=None):
        if when is None:
            remote(src, dst, out, sem, dev).start()
        else:
            pl.when(when)(lambda: remote(src, dst, out, sem, dev).start())

    def arrived(dst, sem):
        remote(dst, dst, out_sem.at[0], sem, sibling).wait_recv()

    def left(src, out):
        remote(src, src, out, in_sem.at[0], sibling).wait_send()

    near = [-1, 1, -2, 2, -3, 3, 4]
    runs = {0: [1, 2, -1, 3, -2, -3, 4], 1: [-1, 1, 2, -2, 3, -3, 4], 2: [-1, 1, -2, 2, 3, -3, 4]}
    block = [zl]
    for i in range(7):
        off = jnp.int32(near[i])
        for at, run in runs.items():
            off = jnp.where(z == at, run[i], jnp.where(z == 15 - at, -run[i], off))
        block.append((zl + off + 8) % 8)

    def block_rows(b, core):
        return pl.multiple_of(b * BW + core * CW, 16)

    def cols(i):
        return pl.ds(pl.multiple_of(block[i] * BW, 128), BW)

    def w_at(start, size):
        return wg.at[pl.ds(pl.multiple_of(start, 16), size), :]

    qkv_in = load(qkv_ref, qkv_v)
    own_heads = load(
        qkv_ref.at[:, pl.ds(0, ROWS), pl.ds(pl.multiple_of(x * GW, 128), GW)], heads.at[:, pl.ds(0, ROWS), :]
    )
    clip_in = load(clip_ref, clip_v)
    conv_in = load(conv_ref, conv_v)
    own_w = load(w_ref, w_at(block_rows(zl, c), CW))
    embed_in = load(embed_ref, embed_v)
    gate_in = load(gate_ref, gate_v)
    hidden_in = load(hidden_ref, hidden_v)

    pl.semaphore_wait(barrier, 8 + jnp.where(z > 0, 1, 0))

    def send_heads(part):
        lo, size = HALVES[part]
        for d in (2, 1, 3):
            send(
                qkv_ref.at[:, pl.ds(0, ROWS), pl.ds(pl.multiple_of(((x + d) % 4) * GW + lo, 128), size)],
                heads.at[:, pl.ds((4 - d) * ROWS, ROWS), pl.ds(lo, size)],
                out_sem.at[0],
                in_sem.at[8 + part],
                at_x(d),
            )

    send_heads(0)
    def own_piece(q, way, when):
        start = ((y + q) % 4) * QR
        send(
            w_ref.at[pl.ds(pl.multiple_of(start, 16), QR), :],
            w_at(block_rows(zl, c) + start, QR),
            out_sem.at[1],
            z_sem.at[way, 2 + q],
            at_z(1 if way == 0 else 15),
            when,
        )

    for r in (0, 1):
        own_piece(r, 0, None)
        own_piece(1 - r, 1, z > 0)
    send(w_ref, w_at(block_rows(zl, c), CW), out_sem.at[1], sib_sem.at[zl], sibling)

    qkv_in.wait()
    tail_rows[...] = jnp.zeros_like(tail_rows)
    for p in range(3):
        last = qkv_v[p, ROWS : ROWS + 1, :].astype(F32)
        for t in range(4 * HG):
            at = (t // HG) * 16 + p * HG + t % HG
            tail_rows[at : at + 1, :] = last[:, t * HD : (t + 1) * HD]
    tail_out[...] = tail_rows[...].astype(BF16)
    for d in (2, 1, 3):
        send(
            tail_out.at[pl.ds(pl.multiple_of(((x + d) % 4) * 16, 16), 16), :],
            tail_in.at[pl.ds((4 - d) * 16, 16), :],
            out_sem.at[8],
            in_sem.at[1],
            at_x(d),
        )
    send_heads(1)

    def w_piece(k, q, way):
        b = (z + (8 - k if way == 0 else k)) % 8
        return w_at(block_rows(b, c) + ((y + q) % 4) * QR, QR), b

    def pass_on(k, q, way, when):
        piece, _ = w_piece(k, q, way)
        send(piece, piece, out_sem.at[1], z_sem.at[way, 2 * k + 2 + q], at_z(1 if way == 0 else 15), when)

    def w_step(k, r, late, only=None):
        todo = []
        for way in (0, 1):
            q = way if r == 0 else 1 - way
            crosses = (z if way == 0 else 15 - z) < k
            here = crosses if late else jnp.logical_not(crosses)
            here = here if only is None else here & only
            piece, b = w_piece(k, q, way)
            pl.when(here)(lambda: arrived(piece, z_sem.at[way, 2 * k + q]))
            if k < 3 or (k == 3 and r == 0):
                pass_on(k, q, way, here & (z > 0) if way == 1 and k < 3 and not late else here)
            todo.append((piece, b, q, here))
        for piece, b, q, here in todo:
            send(piece, piece, out_sem.at[1], y_sem.at[q, b], at_y(1 if q == 0 else 3), here)
            send(piece, piece, out_sem.at[1], sib_sem.at[b], sibling, here)

    def w_back():
        for q in (1, 0):
            own_piece(q, 1, z == 0)
        for k in (1, 2):
            for q in (1, 0):
                pass_on(k, q, 1, z == 0)

    def y_near(i):
        for q, d in ((0, 3), (1, 2)):
            piece = w_at(block_rows(block[i], c) + ((y + d) % 4) * QR, QR)
            arrived(piece, y_sem.at[q, block[i]])
            send(piece, piece, out_sem.at[1], sib_sem.at[block[i]], sibling)

    clip_in.wait()
    conv_in.wait()
    raw = clip_v[...].astype(F32)
    act[:, 0:14, :] = raw / (1.0 + jnp.exp(-raw))
    act[:, 14:16, :] = jnp.zeros((14, 2, 512), F32)
    flat = act[...].reshape(224, 512)
    for k, value in enumerate((pltpu.roll(flat, 1, 0), flat, pltpu.roll(flat, 223, 0))):
        sh[k, 0:16, :] = jnp.zeros((16, 512), BF16)
        sh[k, 240:256, :] = jnp.zeros((16, 512), BF16)
        sh[k, 16:240, :] = value.astype(BF16)
    total = jnp.zeros((224, 128), F32)
    for dy in range(3):
        for dx in range(3):
            taps = jnp.concatenate([conv_v[1, dy, dx]] * 4 + [conv_v[0, dy, dx]] * 4, axis=0)
            total += lax.dot_general(sh[dx, dy * 16 : dy * 16 + 224, :], taps, NT, preferred_element_type=F32)
    cell = lax.broadcasted_iota(jnp.int32, (224, 128), 0)
    lane = lax.broadcasted_iota(jnp.int32, (224, 128), 1)
    parity = ((cell >> 4) & 1) * 2 + (cell & 1)
    spread = jnp.where(((lane >> 4) & 3) == parity, total, 0.0)
    token = lax.broadcasted_iota(jnp.int32, (64, 224), 0)
    cell = lax.broadcasted_iota(jnp.int32, (64, 224), 1)
    mine = (token == (cell >> 5) * 7 + ((cell & 15) >> 1)) & ((cell & 15) < 14)
    both = jnp.dot(
        mine.astype(F32), spread, precision=lax.Precision.HIGHEST, preferred_element_type=F32
    )
    low = lax.broadcasted_iota(jnp.int32, (32, 128), 1) < 64
    this_tap = jnp.where(low, both[0:32], pltpu.roll(both[32:64], 64, 1))
    bsend[...] = jnp.where(low, pltpu.roll(both[0:32], 64, 1), both[32:64])
    send(bsend, brecv, out_sem.at[2], in_sem.at[2], at_x(1))

    w_step(1, 0, False)
    w_step(1, 1, False)
    gate_in.wait()
    hot = lax.broadcasted_iota(jnp.int32, (16, 35), 1) == step_ref[...]
    gate_row[...] = jnp.dot(hot.astype(F32).astype(BF16), gate_v[...], preferred_element_type=F32)

    w_step(2, 0, False)

    own_heads.wait()
    arrived(tail_in.at[pl.ds(16, 48), :], in_sem.at[1])
    tail_in[0:16, :] = tail_out[pl.ds(pl.multiple_of(x * 16, 16), 16), :]
    tail_rows[...] = tail_in[...].astype(F32)
    row = lax.broadcasted_iota(jnp.int32, (16, HD), 0)
    for p in range(3):
        for t in range(HG):
            value = jnp.zeros((16, HD), F32)
            for j in range(4):
                at = j * 16 + p * HG + t
                value = jnp.where(row == j, tail_rows[at : at + 1, :], value)
            heads[p, MAIN:ALL, t * HD : (t + 1) * HD] = value.astype(BF16)
    key_col = lax.broadcasted_iota(jnp.int32, (ALL, ALL), 1)

    def attend(part):
        lo, size = HALVES[part]
        arrived(heads.at[:, pl.ds(ROWS, 3 * ROWS), pl.ds(lo, size)], in_sem.at[8 + part])
        for h in range(lo // HD, (lo + size) // HD):
            at = slice(h * HD, (h + 1) * HD)
            scores = lax.dot_general(heads[0, :, at], heads[1, :, at], NT, preferred_element_type=F32)
            scores = jnp.where(key_col < 196, scores * (1.0 / math.sqrt(HD)), -1e30)
            powers = jnp.exp(scores - jnp.max(scores, axis=1, keepdims=True))
            weights = (powers / jnp.sum(powers, axis=1, keepdims=True)).astype(BF16)
            att[:, at] = jnp.dot(weights, heads[2, :, at], preferred_element_type=F32).astype(BF16)

    tsend[:, 40:48, :] = jnp.zeros((4, 8, 128), F32)

    def halves(i):
        return HALVES if i % 2 == 0 else HALVES[::-1]

    def project(i):
        arrived(w_at(block_rows(block[i], 1 - c), CW), sib_sem.at[block[i]])
        rows = pl.ds(pl.multiple_of(block[i] * BW, 16), BW)
        value = lax.dot_general(att[...], wg[rows, :], NT, preferred_element_type=F32)
        terms[i] = value[0:MAIN].astype(BF16)
        for j in range(4):
            for t in range(5):
                tsend[j, i * 5 + t : i * 5 + t + 1, :] = value[MAIN + j : MAIN + j + 1, t * 128 : (t + 1) * 128]
        if i not in CROSSING:
            for d in (1, 3, 2):
                send(terms.at[i, pl.ds(d * ROWS, ROWS), :], recv.at[4 - d, i], out_sem.at[3], term_sem.at[i], at_x(d))
            return
        for way, (lo, size) in enumerate(halves(i)):
            send(
                terms.at[i, pl.ds(2 * ROWS, ROWS), pl.ds(lo, size)],
                cross.at[i, :, pl.ds(lo, size)],
                out_sem.at[3],
                cross_sem.at[i],
                at_x(1 if way == 0 else 3),
            )

    def add_on(i):
        arrived(cross.at[i], cross_sem.at[i])
        for way, (lo, size) in enumerate(halves(i)):
            d = 1 if way == 0 else 3
            mine = terms[i, d * ROWS : (d + 1) * ROWS, lo : lo + size].astype(F32)
            terms[i, d * ROWS : (d + 1) * ROWS, lo : lo + size] = (
                mine + cross[i, :, lo : lo + size].astype(F32)
            ).astype(BF16)
            send(terms.at[i, pl.ds(d * ROWS, ROWS), :], recv.at[4 - d, i], out_sem.at[3], term_sem.at[i], at_x(d))

    def pass_frame():
        arrived(brecv, in_sem.at[2])
        packs[y, zh] = (this_tap + jnp.where(x > 0, brecv[...], 0.0)).astype(BF16)
        for way, here in ((0, z < 8), (1, z >= 8)):
            send(packs.at[y, way], midway.at[way], out_sem.at[4], in_sem.at[3 + way], at_z(4 if way == 0 else 12), here)

    def pass_far():
        here = (z >= 4) & (z < 12)
        for way in (0, 1):
            pl.when(here)(lambda: arrived(midway.at[way], in_sem.at[3 + way]))
            send(midway.at[way], packs.at[y, way], out_sem.at[5], in_sem.at[5], at_z(4 if way == 0 else 12), here)

    def pass_patches():
        arrived(packs.at[y, 1 - zh], in_sem.at[5])
        for d in (1, 3, 2):
            send(packs.at[y], packs.at[y], out_sem.at[6], in_sem.at[6], at_y(d))

    def choose_patches():
        arrived(packs.at[pl.ds(0, 3)], in_sem.at[6])
        chosen = jnp.zeros((32, 128), F32)
        for k in range(8):
            chosen = jnp.where(source_ref[...] == k, packs[k % 4, k // 4].astype(F32), chosen)
        patch[0:32, :] = chosen.astype(BF16)
        patch[32:64, :] = pltpu.roll(chosen, 64, 1).astype(BF16)

    def finish(i):
        at = cols(i)
        peers = (1, 3) if i in CROSSING else (1, 2, 3)
        arrived(recv.at[pl.ds(0, len(peers)), i], term_sem.at[i])
        projected = terms[i, 0:ROWS, :].astype(F32)
        for d in peers:
            projected += recv[d, i].astype(F32)
        last = jnp.concatenate([tail_sum[i * 5 + t : i * 5 + t + 1, :] for t in range(5)], axis=1)
        projected = jnp.concatenate([projected, last], axis=0)
        condition = jnp.dot(patch[:, 0:64], embed_v[:, at], preferred_element_type=F32)[0 : ROWS + 1]
        out_v[i] = (
            hidden_v[:, at].astype(F32) + reset_ref[...].astype(F32) * condition + gate_row[0:1, at] * projected
        ).astype(BF16)
        copy = pltpu.make_async_copy(out_v.at[i], out_ref.at[:, at], loc_sem.at[len(locals_)])
        copy.start()

    def send_tails(lo, size, k):
        tail_terms[:, lo : lo + size, :] = tsend[:, lo : lo + size, :].astype(BF16)
        for d in (1, 3, 2):
            send(
                tail_terms.at[d, pl.ds(lo, size), :],
                trecv.at[4 - d, pl.ds(lo, size), :],
                out_sem.at[7],
                in_sem.at[k],
                at_x(d),
            )

    def sum_tails(lo, size, k):
        arrived(trecv.at[pl.ds(1, 3), pl.ds(lo, size), :], in_sem.at[k])
        value = tsend[0, lo : lo + size, :]
        for d in (1, 2, 3):
            value += trecv[d, lo : lo + size, :].astype(F32)
        tail_sum[lo : lo + size, :] = value

    attend(0)
    y_near(1)
    w_step(2, 1, False)
    w_step(1, 0, True)
    w_back()
    attend(1)
    own_w.wait()
    edge = jnp.minimum(z, 15 - z)
    project(0)
    w_step(3, 0, False)
    pass_frame()
    w_step(1, 1, True)
    y_near(2)
    w_step(2, 0, True, z != 0)
    project(1)
    w_step(3, 1, False)
    w_step(2, 0, True, z == 0)
    w_step(2, 1, True)
    y_near(3)
    w_step(3, 0, True, edge >= 2)
    project(2)
    w_step(4, 0, False)
    w_step(3, 0, True, edge < 2)
    y_near(4)
    w_step(3, 1, True)
    project(3)
    y_near(5)
    w_step(4, 0, True)
    project(4)
    pass_far()
    add_on(3)
    y_near(6)
    project(5)
    add_on(4)
    y_near(7)
    project(6)
    add_on(5)
    send_tails(0, 32, 7)
    project(7)
    send_tails(32, 16, 10)
    add_on(6)
    pass_patches()
    choose_patches()
    embed_in.wait()
    hidden_in.wait()
    sum_tails(0, 32, 7)
    finish(0)
    finish(1)
    finish(2)
    finish(3)
    finish(4)
    finish(5)
    sum_tails(32, 16, 10)
    finish(6)
    finish(7)
    left(w_at(0, 9 * ROWS), out_sem.at[0])
    left(w_at(0, CW + 56 * QR), out_sem.at[1])
    left(bsend, out_sem.at[2])
    left(w_at(0, NB * 3 * ROWS), out_sem.at[3])
    left(packs.at[y, zh], out_sem.at[4])
    pl.when((z >= 4) & (z < 12))(lambda: left(midway, out_sem.at[5]))
    left(packs.at[pl.ds(0, 3)], out_sem.at[6])
    left(trecv.at[pl.ds(1, 3)], out_sem.at[7])
    left(tail_in.at[pl.ds(16, 48), :], out_sem.at[8])
    pltpu.make_async_copy(out_v, out_v, loc_sem.at[len(locals_)]).wait()


def per_device(qkv, hidden_in, clips, reset, source_group, step_index, conv_weight, embed_weight, out_weight, gate_table):
    anywhere = pl.BlockSpec(memory_space=pl.ANY)
    dma = pltpu.SemaphoreType.DMA
    result = pl.pallas_call(
        body,
        out_shape=jax.ShapeDtypeStruct((49, D), BF16),
        in_specs=[pl.BlockSpec(memory_space=pltpu.VMEM)] * 3 + [anywhere] * 7,
        out_specs=anywhere,
        scratch_shapes=[
            pltpu.VMEM((3, 49, 4 * GW), BF16),
            pltpu.VMEM((49, D), BF16),
            pltpu.VMEM((14, 14, 512), BF16),
            pltpu.VMEM((2, 3, 3, 16, 512), BF16),
            pltpu.VMEM((64, D), BF16),
            pltpu.VMEM((35, D), BF16),
            pltpu.VMEM((NB, 49, BW), BF16),
            pltpu.VMEM((D, GW), BF16),
            pltpu.VMEM((3, ALL, GW), BF16),
            pltpu.VMEM((64, HD), F32),
            pltpu.VMEM((64, HD), BF16),
            pltpu.VMEM((64, HD), BF16),
            pltpu.VMEM((ALL, GW), BF16),
            pltpu.VMEM((NB, MAIN, BW), BF16),
            pltpu.VMEM((NB, ROWS, BW), BF16),
            pltpu.VMEM((4, NB, ROWS, BW), BF16),
            pltpu.VMEM((4, 48, 128), F32),
            pltpu.VMEM((4, 48, 128), BF16),
            pltpu.VMEM((4, 48, 128), BF16),
            pltpu.VMEM((48, 128), F32),
            pltpu.VMEM((14, 16, 512), F32),
            pltpu.VMEM((3, 256, 512), BF16),
            pltpu.VMEM((32, 128), F32),
            pltpu.VMEM((32, 128), F32),
            pltpu.VMEM((4, 2, 32, 128), BF16),
            pltpu.VMEM((2, 32, 128), BF16),
            pltpu.VMEM((16, D), F32),
            pltpu.VMEM((64, 128), BF16),
            dma((9,)),
            dma((9,)),
            dma((2, 10)),
            dma((2, 8)),
            dma((8,)),
            dma((NB,)),
            dma((NB,)),
            dma((11,)),
        ],
        compiler_params=pltpu.CompilerParams(
            collective_id=0, has_side_effects=True, vmem_limit_bytes=48 * 1024 * 1024
        ),
        cost_estimate=pl.CostEstimate(flops=2_000_000_000, bytes_accessed=8_000_000, transcendentals=400_000),
    )(
        reset.reshape(1, 1),
        source_group.reshape(1, 1),
        step_index.reshape(1, 1),
        *(
            pltpu.with_memory_space_constraint(operand, pltpu.HBM)
            for operand in (
                qkv[0].transpose(1, 0, 2),
                hidden_in[0],
                clips[0, 0],
                conv_weight.transpose(0, 1, 2, 4, 3),
                embed_weight,
                out_weight.T,
                gate_table,
            )
        )
    )
    return result[None]


def solution(mesh):
    placed = (
        P(("dp", "shard"), "seq", None, None),
        P(("dp", "shard"), "seq", None),
        P(("dp", "shard"), "seq", None, None, None),
        P(("dp", "shard")),
        P(("dp", "shard")),
        P(("dp", "shard")),
        P(),
        P(),
        P("seq", "shard"),
        P(),
    )
    return jax.shard_map(
        per_device,
        mesh=mesh,
        in_specs=placed,
        out_specs=P(("dp", "shard"), "seq", None),
        check_vma=False,
    )
```
